128 devices in a mesh: seq: 64 (over x, y, z), head: 2 (over core).
Axes of the slice: x: 4, y: 4, z: 4, core: 2. Of those that a mesh axis runs over, the one named last changes fastest.
Arguments:
- ref_queries: bfloat16 [64, 64, 128], P('seq', 'head'), as said below
- query_pos: int32 [64], P('seq'), may hold values from 32768 to 131071
- cache_keys: bfloat16 [131072, 8, 128], P('seq', 'head'), may hold values from -6 to 6
- cache_values: bfloat16 [131072, 8, 128], P('seq', 'head'), may hold values from -6 to 6
- kept_index: int32 [8, 512], P('head'), may hold values from 0 to 131071
Outputs:
- reference_out: bfloat16 [64, 64, 128], P('seq', 'head')
- fitted_values: float32 [8, 512, 128], P('head', 'seq')
The draws below stay inside these ranges and needn't reach their ends.
Inputs may be any that keep to these rules, and one draw needn't show every extreme that they name: `kept_index`: cache positions of the kept rows, repeats possible. `ref_queries`: query vectors of order one or larger.
All inputs are finite; a program needn't handle non-finite values.
Results may differ from the reference program's by a relative error of at most 0.01325.
Values may be sent and summed in bfloat16 or wider, within the bound.
No kernel may reach another device: no remote copies, remote signals or barrier semaphores. Data moves between devices by JAX's collectives and lax.ppermute only.
A program may use at most 192 MiB of HBM per device.

```python
import math
import jax
import jax.numpy as jnp
from jax import lax

D_HEAD = 128
KV_HEADS = 8
HQ = 64
KEPT = 512
S = 131072
R = 64


def draw_ref_queries(key, part):
    key = jax.random.fold_in(key, 7)
    shape_all = (R, HQ, D_HEAD)
    values_drawn = 3.0 * jax.random.normal(key, shape_all, jnp.float32)
    return values_drawn.astype(jnp.bfloat16)


def draw_cache_keys(key, part):
    key = jax.random.fold_in(key, 11)
    freq_key = jax.random.fold_in(key, 1)
    phase_key = jax.random.fold_in(key, 2)
    amp_key = jax.random.fold_in(key, 3)
    noise_key = jax.random.fold_in(key, 4)
    channel_shape = (KV_HEADS, D_HEAD)
    frequency = jnp.exp(jax.random.uniform(freq_key, channel_shape, jnp.float32, 0.0, math.log(KEPT / 2.0)))
    phase = jax.random.uniform(phase_key, channel_shape, jnp.float32, 0.0, 1.0)
    amplitude = jnp.exp(jax.random.uniform(amp_key, channel_shape, jnp.float32, math.log(0.3), math.log(1.5)))
    position = (jnp.arange(S, dtype=jnp.int32).astype(jnp.float32) / S)[:, None, None]
    cycle = jnp.mod(position * frequency[None] + phase[None], 1.0)
    smooth = 1.27 * amplitude[None] * jnp.cos(2.0 * math.pi * cycle)
    noise = 0.45 * jax.random.normal(noise_key, (S, KV_HEADS, D_HEAD), jnp.float32)
    return jnp.clip(smooth + noise, -6.0, 6.0).astype(jnp.bfloat16)


def place_ends(array, own_key, low, largest):
    extent = array.shape
    spot = [jax.random.randint(jax.random.fold_in(own_key, axis), (), 0, extent[axis]) for axis in range(len(extent))]
    array = array.at[tuple(spot)].set(low)
    longest = extent.index(max(extent))
    spot[longest] = (spot[longest] + 1) % extent[longest]
    return array.at[tuple(spot)].set(largest)


def levels(key, shape, split, least, top_value):
    factor_of = 1.0
    for dim, parts in split:
        heights = jax.random.uniform(jax.random.fold_in(jax.random.fold_in(key, 6), dim), (parts,), jnp.float32, least / len(split), top_value / len(split))
        factor_of = factor_of * jnp.repeat(jnp.exp(heights), shape[dim] // parts).reshape((-1,) + (1,) * (len(shape) - 1 - dim))
    return factor_of


def bell_draw(key, shape, width, reach, shards=(), held_as=jnp.bfloat16):
    entries = width * jax.random.normal(key, shape, jnp.float32)
    if shards:
        entries = entries * levels(key, shape, shards, -0.22, 0.18)
    return jnp.clip(entries, -reach, reach).astype(held_as)


def setup_inputs(seed: int = 0) -> dict:
    splits = jax.random.split(jax.random.key(seed), 6)
    return {
        "ref_queries": draw_ref_queries(jax.random.fold_in(splits[5], 71), 0),
        "query_pos": place_ends(jax.random.randint(splits[1], (R,), S // 4, S), jax.random.fold_in(splits[1], 1), S // 4, S - 1).astype(jnp.int32),
        "cache_keys": draw_cache_keys(jax.random.fold_in(splits[5], 71), 0),
        "cache_values": bell_draw(splits[3], (S, KV_HEADS, D_HEAD), 1.0, 6.0, ((0, 64), (1, 2))),
        "kept_index": place_ends(jax.random.randint(splits[4], (KV_HEADS, KEPT), 0, S), jax.random.fold_in(splits[4], 1), 0, S - 1).astype(jnp.int32),
    }


ridge_weight = 0.01
neg_floor = -1e+30

def reference(ref_queries, query_pos, cache_keys, cache_values, kept_index):
    total_pos = cache_keys.shape[0]
    group_size = HQ // KV_HEADS
    scaling_factor = D_HEAD ** (-0.5)
    key_pos = jnp.arange(total_pos, dtype=jnp.int32)
    keys_f32 = cache_keys.astype(jnp.float32)
    values_f32 = cache_values.astype(jnp.float32)

    def attend_block(inputs):
        queries, positions = inputs
        query_f32 = queries.astype(jnp.float32).reshape(-1, KV_HEADS, group_size, D_HEAD)
        attention_scores = jnp.einsum('bhgd,shd->bhgs', query_f32, keys_f32) * scaling_factor
        allowed = (key_pos[None, :] <= positions[:, None])[:, None, None, :]
        attention_scores = jnp.where(allowed, attention_scores, neg_floor)
        weights = jax.nn.softmax(attention_scores, axis=-1)
        return jnp.einsum('bhgs,shd->bhgd', weights, values_f32)
    attended = lax.map(attend_block, (ref_queries.reshape(R // 8, 8, HQ, D_HEAD), query_pos.reshape(R // 8, 8)))
    attended = attended.reshape(R, KV_HEADS, group_size, D_HEAD)
    reference_out = attended.reshape(R, HQ, D_HEAD).astype(jnp.bfloat16)
    head_iota = jnp.arange(KV_HEADS, dtype=jnp.int32)[:, None]
    retained_key_rows = cache_keys[kept_index, head_iota]
    kept_vals = cache_values[kept_index, head_iota]
    grouped_heads_view = ref_queries.astype(jnp.float32).reshape(R, KV_HEADS, group_size, D_HEAD)
    attention_scores = jnp.einsum('jfal,fwl->fjaw', grouped_heads_view, retained_key_rows.astype(jnp.float32)) * scaling_factor
    mixing_weights = jax.nn.softmax(attention_scores, axis=-1).reshape(KV_HEADS, R * group_size, KEPT)
    target_outputs = attended.transpose(1, 0, 2, 3).reshape(KV_HEADS, R * group_size, D_HEAD)
    gram_matrix = jnp.einsum('hkm,hkn->hmn', mixing_weights, mixing_weights, precision=lax.Precision.HIGHEST)
    cross_products_matrix = jnp.einsum('jze,jzv->jev', mixing_weights, target_outputs, precision=lax.Precision.HIGHEST)
    left_side = gram_matrix + ridge_weight * jnp.eye(KEPT, dtype=jnp.float32)
    right_side = cross_products_matrix + ridge_weight * kept_vals.astype(jnp.float32)
    lower_factor = jnp.linalg.cholesky(left_side)

    def solve_head(lower_part, right_part):
        inner_part = jax.scipy.linalg.solve_triangular(lower_part, right_part, lower=True)
        return jax.scipy.linalg.solve_triangular(lower_part, inner_part, lower=True, trans=1)
    fitted_values = jax.vmap(solve_head)(lower_factor, right_side)
    return (reference_out, fitted_values)
```

```python
import functools
import math

import jax
import jax.numpy as jnp
from jax import lax
from jax.experimental import pallas as pl
from jax.experimental.pallas import tpu as pltpu
from jax.sharding import Mesh, PartitionSpec as P

ridge_weight = 0.01
masked_score = -1e30
highest = lax.Precision.HIGHEST
f32 = jnp.float32
bf16 = jnp.bfloat16

seq_axes = ("x", "y", "z")
count_rows = 64
heads_here = 4
group = 8
width = 128
local_len = 2048
kept = 512
chunk = 512
scale = width ** (-0.5)
scale_log2 = scale * math.log2(math.e)


def params(mib=56, **more):
    return pltpu.CompilerParams(vmem_limit_bytes=mib * 2**20, **more)


def call(kernel, name, out_shape, **more):
    if "compiler_params" not in more:
        more["compiler_params"] = params()
    return pl.pallas_call(kernel, name=name, out_shape=out_shape, **more)


def shape(dims, dtype):
    return jax.ShapeDtypeStruct(dims, dtype)


whole_vmem = pl.BlockSpec(memory_space=pltpu.VMEM)
whole_smem = pl.BlockSpec(memory_space=pltpu.SMEM)


def prepare_kernel(index_ref, keys_ref, values_ref, both_ref, packet_ref, wide, spread, total):
    step = pl.program_id(0)

    @pl.when(step == 0)
    def _():
        for h in range(heads_here):
            row = jnp.broadcast_to(index_ref[h : h + 1, :], (width, kept))
            spread[h] = row.T

    lane = lax.broadcasted_iota(jnp.int32, (kept, width), 1)
    wide[0] = keys_ref[...].astype(f32)
    wide[1] = values_ref[...].astype(f32)
    for h in range(heads_here):
        rows_k = wide[0, pl.ds(h, chunk, stride=heads_here), :].astype(bf16)
        rows_v = wide[1, pl.ds(h, chunk, stride=heads_here), :].astype(bf16)
        rows = jnp.concatenate([rows_k, rows_v], 1)
        both_ref[h] = rows
        wanted = spread[h] - step * chunk
        hot = jnp.concatenate(
            [
                jnp.where(wanted == lane + g * width, 1.0, 0.0).astype(bf16)
                for g in range(chunk // width)
            ],
            1,
        )
        found = jnp.dot(hot, rows, preferred_element_type=f32)

        @pl.when(step == 0)
        def _():
            total[h] = found

        @pl.when(step > 0)
        def _():
            total[h] += found

    @pl.when(step == local_len // chunk - 1)
    def _():
        for h in range(heads_here):
            packet_ref[16 * h : 16 * h + 16] = total[h].reshape(16, 32, 2 * width).astype(bf16)


def prepare(local_index, keys, values):
    rows = chunk * heads_here
    return call(
        prepare_kernel,
        "prepare",
        (
            shape((heads_here, local_len, 2 * width), bf16),
            shape((count_rows, 32, 2 * width), bf16),
        ),
        grid=(local_len // chunk,),
        in_specs=[
            pl.BlockSpec((heads_here, kept), lambda i: (0, 0)),
            pl.BlockSpec((rows, width), lambda i: (i, 0)),
            pl.BlockSpec((rows, width), lambda i: (i, 0)),
        ],
        out_specs=[
            pl.BlockSpec((heads_here, chunk, 2 * width), lambda i: (0, i, 0)),
            pl.BlockSpec((count_rows, 32, 2 * width), lambda i: (0, 0, 0)),
        ],
        scratch_shapes=[
            pltpu.VMEM((2, rows, width), f32),
            pltpu.VMEM((heads_here, kept, width), jnp.int32),
            pltpu.VMEM((heads_here, kept, 2 * width), f32),
        ],
        cost_estimate=pl.CostEstimate(
            flops=2 * 2 * 512 * 2048 * 256 * 4, bytes_accessed=12 * 2**20, transcendentals=0
        ),
    )(local_index, keys, values)


def attend_kernel(base_ref, queries_ref, both_ref, packet_ref, keys, values):
    h = pl.program_id(0)
    lane = lax.broadcasted_iota(jnp.int32, (local_len, width), 1)

    @pl.when(h == 0)
    def _():
        pieces = queries_ref[:, heads_here].astype(f32)
        row_id = lax.broadcasted_iota(jnp.int32, (count_rows, width), 0)
        lane_id = lax.broadcasted_iota(jnp.int32, (count_rows, width), 1)
        place = pieces[:, 0] + 256.0 * pieces[:, 1] + 65536.0 * pieces[:, 2]
        place = jnp.sum(jnp.where(row_id == lane_id, place, 0.0), axis=0, keepdims=True)
        spot = lax.broadcasted_iota(jnp.int32, (local_len, width), 0) + base_ref[0]
        late = (spot.astype(f32) > place) & (lane < count_rows)
        keys[:, width:] = jnp.where(late, masked_score, 0.0).astype(bf16)
        values[:, width:] = jnp.where(lane == 0, 1.0, 0.0).astype(bf16)

    keys[:, :width] = both_ref[0, :, :width]
    values[:, :width] = both_ref[0, :, width:]
    q = queries_ref[:, h].astype(f32).reshape(count_rows * group, width)
    tile = 256
    lane_t = lax.broadcasted_iota(jnp.int32, (tile, width), 1)
    row_t = lax.broadcasted_iota(jnp.int32, (tile, width), 0)
    for part in range(count_rows * group // tile):
        own = jnp.where(row_t // group + part * (tile // group) == lane_t, 1.0, 0.0)
        q_part = jnp.concatenate([q[part * tile : (part + 1) * tile], own], 1).astype(bf16)
        s = lax.dot_general(
            q_part, keys[...], (((1,), (1,)), ((), ())), preferred_element_type=f32
        )
        peak = jnp.max(s, axis=1, keepdims=True)
        w = jnp.exp2((s - peak) * scale_log2).astype(bf16)
        o = jnp.dot(w, values[...], preferred_element_type=f32)
        sums = o[:, width : width + 1]
        mass = peak * scale_log2 + jnp.log2(sums)
        high = mass.astype(bf16).astype(f32)
        middle = (mass - high).astype(bf16).astype(f32)
        low = mass - high - middle
        side = jnp.where(
            lane_t == 0,
            high,
            jnp.where(lane_t == 1, middle, jnp.where(lane_t == 2, low, 0.0)),
        )
        done = jnp.concatenate([o[:, :width] / sums, side], 1)
        rows = tile // group
        packet_ref[part * rows : (part + 1) * rows, 0] = done.reshape(
            rows, group, 2 * width
        ).astype(bf16)


def attend(base, queries, both):
    return call(
        attend_kernel,
        "attend",
        shape((count_rows, heads_here, group, 2 * width), bf16),
        grid=(heads_here,),
        in_specs=[
            whole_smem,
            pl.BlockSpec((count_rows, heads_here + 1, group, width), lambda h: (0, 0, 0, 0)),
            pl.BlockSpec((1, local_len, 2 * width), lambda h: (h, 0, 0)),
        ],
        out_specs=pl.BlockSpec((count_rows, 1, group, 2 * width), lambda h: (0, h, 0, 0)),
        scratch_shapes=[
            pltpu.VMEM((local_len, 2 * width), bf16),
            pltpu.VMEM((local_len, 2 * width), bf16),
        ],
        cost_estimate=pl.CostEstimate(
            flops=2 * 2 * 512 * 2048 * 256 * 4,
            bytes_accessed=6 * 2**20,
            transcendentals=4 * 512 * 2048,
        ),
    )(base, queries, both)


def combine_kernel(parts_ref, out_ref, spread_ref):
    for h in range(heads_here):
        part = parts_ref[:, h].astype(f32)
        mass = jnp.sum(part[:, :, width:], axis=2, keepdims=True)
        top = jnp.max(mass, axis=0, keepdims=True)
        share = jnp.exp2(mass - top)
        full = jnp.sum(share * part[:, :, :width], axis=0) / jnp.sum(share, axis=0)
        out_ref[h] = full.astype(bf16)
        spread_ref[16 * h : 16 * h + 16] = jnp.broadcast_to(full[None], (16, group, width))


def combine(parts):
    return call(
        combine_kernel,
        "combine",
        (shape((heads_here, group, width), bf16), shape((count_rows, group, width), f32)),
        cost_estimate=pl.CostEstimate(
            flops=2 * 2**20, bytes_accessed=2 * 2**20, transcendentals=2048
        ),
    )(parts)


def gather_kernel(parts_ref, out_ref):
    found = jnp.sum(parts_ref[...].astype(f32), axis=0).astype(bf16)
    out_ref[...] = jnp.broadcast_to(found[None], out_ref.shape)


def add_kept(parts):
    return call(
        gather_kernel,
        "add_kept",
        shape((16, 32, 2 * width), bf16),
        cost_estimate=pl.CostEstimate(flops=2**20, bytes_accessed=2**20, transcendentals=0),
    )(parts)


def reciprocal(x):
    r = pl.reciprocal(x, approx=True)
    r = r * (2.0 - x * r)
    return r * (2.0 - x * r)


def invert_small(d, n):
    if n == 1:
        return [[reciprocal(d[0][0])]]
    if n == 2:
        r = reciprocal(d[0][0] * d[1][1] - d[0][1] * d[0][1])
        off = -d[0][1] * r
        return [[d[1][1] * r, off], [off, d[0][0] * r]]
    h = n // 2
    side = range(h)
    p = [[d[i][j] for j in side] for i in side]
    q = [[d[i][h + j] for j in side] for i in side]
    pin = invert_small(p, h)
    pq = [[sum(pin[i][k] * q[k][j] for k in side) for j in side] for i in side]
    t = [[None] * h for _ in side]
    for i in side:
        for j in range(i, h):
            t[i][j] = t[j][i] = d[h + i][h + j] - sum(q[k][i] * pq[k][j] for k in side)
    tin = invert_small(t, h)
    pqt = [[sum(pq[i][k] * tin[k][j] for k in side) for j in side] for i in side]
    out = [[None] * n for _ in range(n)]
    for i in side:
        for j in side:
            out[h + i][h + j] = tin[i][j]
            out[i][h + j] = -pqt[i][j]
            out[h + j][i] = -pqt[i][j]
    for i in side:
        for j in range(i, h):
            out[i][j] = out[j][i] = pin[i][j] + sum(pqt[i][k] * pq[j][k] for k in side)
    return out


def invert_block(a, n, b, h):
    lane = lax.broadcasted_iota(jnp.int32, (8, n), 1)
    sub = lax.broadcasted_iota(jnp.int32, (8, n), 0)
    lane_n = lax.broadcasted_iota(jnp.int32, (n, n), 1)
    for first in range(0, n, h):
        tiles = [a[first + 8 * i : first + 8 * i + 8, :] for i in range(h // 8)]
        for k in range(first, first + h, b):
            at, off = (k - first) // 8, k % 8
            rows = [
                jnp.broadcast_to(tiles[at][off + s : off + s + 1, :], (8, n)) for s in range(b)
            ]
            d = [[None] * b for _ in range(b)]
            for s in range(b):
                for t in range(s, b):
                    d[s][t] = d[t][s] = jnp.broadcast_to(rows[s][:, k + t : k + t + 1], (8, n))
            columns = [
                [jnp.broadcast_to(tile[:, k + s : k + s + 1], (8, n)) for tile in tiles]
                for s in range(b)
            ]
            inverse = invert_small(d, b)
            inside = (lane >= k) & (lane < k + b)
            rows = [
                jnp.where(lane == k + s, 1.0, jnp.where(inside, 0.0, rows[s])) for s in range(b)
            ]
            new = [sum(inverse[s][t] * rows[t] for t in range(b)) for s in range(b)]
            after = []
            for i, tile in enumerate(tiles):
                left = jnp.where(inside, 0.0, tile)
                left = left - sum(columns[s][i] * new[s] for s in range(b))
                if i == at:
                    for s in range(b):
                        left = jnp.where(sub == off + s, new[s], left)
                after.append(left)
            tiles = after
        r = jnp.concatenate(tiles, 0)
        inside_n = (lane_n >= first) & (lane_n < first + h)
        rest = jnp.where(inside_n, 0.0, a) - jnp.dot(
            a[:, first : first + h], r, precision=highest, preferred_element_type=f32
        )
        pieces = ([rest[:first]] if first else []) + [r]
        a = jnp.concatenate(pieces + ([rest[first + h :]] if first + h < n else []), 0)
    return a


def fit_kernel(place_ref, queries_ref, kept_ref, weight_ref, plain_ref, mixing, a):
    n = 128
    head, own = place_ref[0], place_ref[1]
    q = queries_ref[:, head].astype(f32).reshape(count_rows * group, width).astype(bf16)
    s = lax.dot_general(
        kept_ref[:, :width], q, (((1,), (1,)), ((), ())), preferred_element_type=f32
    )
    e = jnp.exp((s - jnp.max(s, axis=0, keepdims=True)) * scale)
    mixing[...] = e / jnp.sum(e, axis=0, keepdims=True)
    m = mixing[...]
    row = lax.broadcasted_iota(jnp.int32, (kept, kept), 0)
    column = lax.broadcasted_iota(jnp.int32, (kept, kept), 1)
    a[...] = lax.dot_general(
        m, m, (((1,), (1,)), ((), ())), precision=highest, preferred_element_type=f32
    ) + jnp.where(row == column, ridge_weight, 0.0)
    eye = jnp.where(row[:n, :n] == column[:n, :n], 1.0, 0.0)

    def step(k, _):
        at = pl.ds(pl.multiple_of(k * n, n), n)
        p = invert_block(a[at, at], n, 4, 32)
        a[at, at] = -eye
        left = a[:, at]
        a[:, at] = jnp.zeros((kept, n), f32)
        a[at, at] = eye
        r = jnp.dot(p, a[at, :], precision=highest, preferred_element_type=f32)
        a[at, :] = jnp.zeros((n, kept), f32)
        a[...] -= jnp.dot(left, r, precision=highest, preferred_element_type=f32)
        return 0

    lax.fori_loop(0, kept // n, step, 0)
    picked = jnp.concatenate(
        [a[pl.ds(pl.multiple_of(128 * i + 8 * own, 8), 8), :] for i in range(4)], 0
    )
    weight_ref[...] = jnp.dot(picked, m, precision=highest, preferred_element_type=f32)
    plain_ref[...] = ridge_weight * jnp.dot(
        picked, kept_ref[:, width:].astype(f32), precision=highest, preferred_element_type=f32
    )


def fit(place, queries, kept_rows):
    return call(
        fit_kernel,
        "fit",
        (shape((32, kept), f32), shape((32, width), f32)),
        in_specs=[whole_smem, whole_vmem, whole_vmem],
        scratch_shapes=[pltpu.VMEM((kept, kept), f32), pltpu.VMEM((kept, kept), f32)],
        cost_estimate=pl.CostEstimate(
            flops=40 * 10**9, bytes_accessed=2 * 2**20, transcendentals=2**18
        ),
    )(place, queries, kept_rows)


def finish_kernel(weight_ref, plain_ref, targets_ref, out_ref):
    targets = targets_ref[...].reshape(count_rows * group, width)
    out = plain_ref[...] + jnp.dot(
        weight_ref[...], targets, precision=highest, preferred_element_type=f32
    )
    out_ref[...] = out.reshape(4, 8, width)


def finish(weight, plain, targets):
    return call(
        finish_kernel,
        "finish",
        shape((4, 8, width), f32),
        cost_estimate=pl.CostEstimate(
            flops=6 * 2 * 32 * 512 * 128, bytes_accessed=2**19, transcendentals=0
        ),
    )(weight, plain, targets)


def on_device(ref_queries, query_pos, cache_keys, cache_values, kept_index):
    at_x, at_y, at_z = (lax.axis_index(a) for a in seq_axes)
    own = at_y * 4 + at_z
    base = ((at_x * 16 + own) * local_len).astype(jnp.int32)
    place = jnp.stack([at_x, own]).astype(jnp.int32)

    at = query_pos[0]
    pieces = jnp.stack([at & 255, (at >> 8) & 255, at >> 16]).astype(bf16)
    pieces = jnp.pad(jnp.broadcast_to(pieces[:, None], (3, width)), ((0, group - 3), (0, 0)))
    packet = jnp.concatenate(
        [ref_queries.reshape(heads_here, group, width), pieces[None]], 0
    )
    queries = lax.all_to_all(
        jnp.broadcast_to(packet[None], (count_rows,) + packet.shape), seq_axes, 0, 0
    )

    both, kept_parts = prepare(
        kept_index - base,
        cache_keys.reshape(local_len * heads_here, width),
        cache_values.reshape(local_len * heads_here, width),
    )
    kept_parts = lax.all_to_all(kept_parts, seq_axes, 0, 0)
    kept_rows = lax.all_to_all(add_kept(kept_parts), ("y", "z"), 0, 0).reshape(kept, 2 * width)

    parts = lax.all_to_all(attend(base[None], queries, both), seq_axes, 0, 0)
    out, targets = combine(parts)
    targets = lax.all_to_all(targets, seq_axes, 0, 0)
    weight, plain = fit(place, queries, kept_rows)
    fitted = lax.all_to_all(finish(weight, plain, targets), "x", 0, 0)
    return (out.reshape(1, heads_here * group, width), fitted)


def solution(mesh):
    split = Mesh(mesh.devices.reshape(4, 4, 4, 2), seq_axes + ("head",))
    in_specs = (
        P(seq_axes, "head", None),
        P(seq_axes),
        P(seq_axes, "head", None),
        P(seq_axes, "head", None),
        P("head", None),
    )
    out_specs = (P(seq_axes, "head", None), P("head", seq_axes, None))
    return jax.shard_map(
        on_device, mesh=split, in_specs=in_specs, out_specs=out_specs, check_vma=False
    )
```

```python
import functools
import math

import jax
import jax.numpy as jnp
from jax import lax
from jax.experimental import pallas as pl
from jax.experimental.pallas import tpu as pltpu
from jax.sharding import Mesh, PartitionSpec as P

ridge_weight = 0.01
masked_score = -1e30
highest = lax.Precision.HIGHEST
f32 = jnp.float32
bf16 = jnp.bfloat16

seq_axes = ("x", "y", "z")
count_rows = 64
heads_here = 4
group = 8
width = 128
local_len = 2048
kept = 512
chunk = 512
slots = 32
panel = 64
early = 1
scale = width ** (-0.5)
scale_log2 = scale * math.log2(math.e)


def params(mib=56, **more):
    return pltpu.CompilerParams(vmem_limit_bytes=mib * 2**20, **more)


def call(kernel, name, out_shape, **more):
    if "compiler_params" not in more:
        more["compiler_params"] = params()
    return pl.pallas_call(kernel, name=name, out_shape=out_shape, **more)


def shape(dims, dtype):
    return jax.ShapeDtypeStruct(dims, dtype)


whole_vmem = pl.BlockSpec(memory_space=pltpu.VMEM)
whole_smem = pl.BlockSpec(memory_space=pltpu.SMEM)


def spread_index():
    at = [lax.axis_index(name) for name in seq_axes]
    return at[0], at[1] * 4 + at[2]


def own_base():
    plane, own = spread_index()
    return (plane * 16 + own) * local_len


def pack_kernel(pos_ref, index_ref, queries_ref, keys_ref, packet_ref, slot, found, crowd):
    step = pl.program_id(0)
    rows = chunk * heads_here

    @pl.when(step == 0)
    def _():
        local = index_ref[...] - own_base()
        inside = (local >= 0) & (local < local_len)
        row_id = lax.broadcasted_iota(jnp.int32, (kept, kept), 0)
        lane_id = lax.broadcasted_iota(jnp.int32, (kept, kept), 1)
        before = jnp.where(row_id < lane_id, 1.0, 0.0).astype(bf16)
        rank = jnp.dot(
            jnp.where(inside, 1.0, 0.0).astype(bf16), before, preferred_element_type=f32
        )
        rank = jnp.where(inside, rank, -1.0)
        most = jnp.max(jnp.max(rank, axis=1, keepdims=True), axis=0, keepdims=True)
        crowd[...] = jnp.broadcast_to(jnp.where(most >= slots - 1.0, 1.0, 0.0), crowd.shape)
        spot = (local * heads_here + 1).astype(f32)
        slot_id = lax.broadcasted_iota(jnp.int32, (slots, kept), 0).astype(f32)
        for h in range(heads_here):
            mine = jnp.where(rank[h : h + 1] == slot_id, spot[h : h + 1] + float(h), 0.0)
            taken = jnp.sum(mine, axis=1, keepdims=True) - 1.0
            slot[h * slots : (h + 1) * slots] = jnp.broadcast_to(taken, (slots, width))
        found[...] = jnp.zeros(found.shape, f32)

    found[...] += jnp.dot(
        one_hot(slot[...] - (step * rows).astype(f32), rows),
        keys_ref[...],
        preferred_element_type=f32,
    )

    @pl.when(step == local_len // chunk - 1)
    def _():
        at = pos_ref[0]
        sub = lax.broadcasted_iota(jnp.int32, (group, width), 0)
        lane = lax.broadcasted_iota(jnp.int32, (group, width), 1)
        pieces = jnp.where(
            lane == 0, at & 255, jnp.where(lane == 1, (at >> 8) & 255, at >> 16)
        ).astype(f32)
        pieces = jnp.where(lane == 3, crowd[...], pieces)
        for h in range(heads_here):
            sent = found[h * slots : (h + 1) * slots].reshape(4, 8, width)
            last = jnp.where(sub == 7, pieces, sent[3])
            full = jnp.concatenate(
                [queries_ref[...].astype(f32), sent[:3], last[None]], 0
            ).astype(bf16)
            packet_ref[16 * h : 16 * h + 16] = jnp.broadcast_to(full[None], (16,) + full.shape)


def one_hot(wanted, size):
    lane = lax.broadcasted_iota(jnp.int32, wanted.shape, 1).astype(wanted.dtype)
    return jnp.concatenate(
        [
            jnp.where(wanted == lane + g * width, 1.0, 0.0).astype(bf16)
            for g in range(size // width)
        ],
        1,
    )


def pack(query_pos, kept_index, queries, keys):
    rows = chunk * heads_here
    return call(
        pack_kernel,
        "pack",
        (
            shape((count_rows, 8, 8, width), bf16),
            shape((heads_here * slots, width), f32),
        ),
        grid=(local_len // chunk,),
        in_specs=[
            whole_smem,
            pl.BlockSpec((heads_here, kept), lambda i: (0, 0)),
            pl.BlockSpec((heads_here, group, width), lambda i: (0, 0, 0)),
            pl.BlockSpec((rows, width), lambda i: (i, 0)),
        ],
        out_specs=[
            pl.BlockSpec((count_rows, 8, 8, width), lambda i: (0, 0, 0, 0)),
            pl.BlockSpec((heads_here * slots, width), lambda i: (0, 0)),
        ],
        scratch_shapes=[
            pltpu.VMEM((heads_here * slots, width), f32),
            pltpu.VMEM((group, width), f32),
        ],
        cost_estimate=pl.CostEstimate(
            flops=2 * 128 * 8192 * 128, bytes_accessed=3 * 2**20, transcendentals=0
        ),
    )(query_pos, kept_index, queries, keys)


def regroup_kernel(slot_ref, keys_ref, values_ref, both_ref, found_ref, wide, found):
    step = pl.program_id(0)
    rows = chunk * heads_here
    wide[0] = keys_ref[...].astype(f32)
    wide[1] = values_ref[...].astype(f32)
    for h in range(heads_here):
        at = pl.ds(h, chunk, stride=heads_here)
        both_ref[h] = jnp.concatenate([wide[0, at, :], wide[1, at, :]], 1).astype(bf16)

    @pl.when(step == 0)
    def _():
        found[...] = jnp.zeros(found.shape, f32)

    found[...] += jnp.dot(
        one_hot(slot_ref[...] - (step * rows).astype(f32), rows),
        values_ref[...],
        preferred_element_type=f32,
    )

    @pl.when(step == local_len // chunk - 1)
    def _():
        found_ref[...] = found[...].reshape(found_ref.shape).astype(bf16)


def regroup(slot, keys, values):
    rows = chunk * heads_here
    return call(
        regroup_kernel,
        "regroup",
        (
            shape((heads_here, local_len, 2 * width), bf16),
            shape((heads_here, 4, 8, width), bf16),
        ),
        grid=(local_len // chunk,),
        in_specs=[
            pl.BlockSpec((heads_here * slots, width), lambda i: (0, 0)),
            pl.BlockSpec((rows, width), lambda i: (i, 0)),
            pl.BlockSpec((rows, width), lambda i: (i, 0)),
        ],
        out_specs=[
            pl.BlockSpec((heads_here, chunk, 2 * width), lambda i: (0, i, 0)),
            pl.BlockSpec((heads_here, 4, 8, width), lambda i: (0, 0, 0, 0)),
        ],
        scratch_shapes=[
            pltpu.VMEM((2, rows, width), f32),
            pltpu.VMEM((heads_here * slots, width), f32),
        ],
        cost_estimate=pl.CostEstimate(
            flops=2 * 128 * 8192 * 128, bytes_accessed=8 * 2**20, transcendentals=0
        ),
    )(slot, keys, values)


def attend_kernel(queries_ref, both_ref, packet_ref, keys, values, side):
    h = pl.program_id(0)
    lane = lax.broadcasted_iota(jnp.int32, (local_len, width), 1)

    @pl.when(h == 0)
    def _():
        pieces = queries_ref[:, 7].astype(f32)[:, 7]
        row_id = lax.broadcasted_iota(jnp.int32, (count_rows, width), 0)
        lane_id = lax.broadcasted_iota(jnp.int32, (count_rows, width), 1)
        place = pieces[:, 0:1] + 256.0 * pieces[:, 1:2] + 65536.0 * pieces[:, 2:3]
        place = jnp.sum(jnp.where(row_id == lane_id, place, 0.0), axis=0, keepdims=True)
        spot = lax.broadcasted_iota(jnp.int32, (local_len, width), 0) + own_base()
        late = (spot.astype(f32) > place) & (lane < count_rows)
        keys[:, width:] = jnp.where(late, masked_score, 0.0).astype(bf16)
        values[:, width:] = jnp.where(lane == 0, 1.0, 0.0).astype(bf16)
        side[...] = jnp.zeros(side.shape, f32)

    keys[:, :width] = both_ref[0, :, :width]
    values[:, :width] = both_ref[0, :, width:]
    q = queries_ref[:, h].astype(f32).reshape(count_rows * group, width)
    tile = 256
    lane_t = lax.broadcasted_iota(jnp.int32, (tile, width), 1)
    row_t = lax.broadcasted_iota(jnp.int32, (tile, width), 0)

    def scores(part):
        own = jnp.where(row_t // group + part * (tile // group) == lane_t, 1.0, 0.0)
        q_part = jnp.concatenate([q[part * tile : (part + 1) * tile], own], 1).astype(bf16)
        return lax.dot_general(
            q_part, keys[...], (((1,), (1,)), ((), ())), preferred_element_type=f32
        )

    parts = count_rows * group // tile
    s = scores(0)
    for part in range(parts):
        after = scores(part + 1) if part + 1 < parts else None
        peak = jnp.max(s, axis=1, keepdims=True)
        w = jnp.exp2((s - peak) * scale_log2).astype(bf16)
        o = jnp.dot(w, values[...], preferred_element_type=f32)
        sums = o[:, width : width + 1]
        mass = peak * scale_log2 + jnp.log2(sums)
        high = mass.astype(bf16).astype(f32)
        middle = (mass - high).astype(bf16).astype(f32)
        low = mass - high - middle
        first = 3 * h
        mark = jnp.where(
            lane_t == first,
            high,
            jnp.where(lane_t == first + 1, middle, jnp.where(lane_t == first + 2, low, 0.0)),
        )
        rows = tile // group
        own = slice(part * rows, (part + 1) * rows)
        side[own] += mark.reshape(rows, group, width)
        packet_ref[own, h] = (o[:, :width] / sums).reshape(rows, group, width).astype(bf16)
        s = after

    @pl.when(h == heads_here - 1)
    def _():
        packet_ref[:, heads_here] = side[...].astype(bf16)


def attend(packets, both):
    return call(
        attend_kernel,
        "attend",
        shape((count_rows, heads_here + 1, group, width), bf16),
        grid=(heads_here,),
        in_specs=[
            pl.BlockSpec((count_rows, 8, group, width), lambda h: (0, 0, 0, 0)),
            pl.BlockSpec((1, local_len, 2 * width), lambda h: (h, 0, 0)),
        ],
        out_specs=pl.BlockSpec(
            (count_rows, heads_here + 1, group, width), lambda h: (0, 0, 0, 0)
        ),
        scratch_shapes=[
            pltpu.VMEM((local_len, 2 * width), bf16),
            pltpu.VMEM((local_len, 2 * width), bf16),
            pltpu.VMEM((count_rows, group, width), f32),
        ],
        cost_estimate=pl.CostEstimate(
            flops=2 * 2 * 512 * 2048 * 256 * 4,
            bytes_accessed=6 * 2**20,
            transcendentals=4 * 512 * 2048,
        ),
    )(packets, both)


def combine_kernel(parts_ref, values_ref, out_ref, spread_ref):
    side = parts_ref[:, heads_here].astype(f32)
    lane = lax.broadcasted_iota(jnp.int32, side.shape, 2)
    for h in range(heads_here):
        part = parts_ref[:, h].astype(f32)
        own = (lane >= 3 * h) & (lane < 3 * h + 3)
        mass = jnp.sum(jnp.where(own, side, 0.0), axis=2, keepdims=True)
        top = jnp.max(mass, axis=0, keepdims=True)
        share = jnp.exp2(mass - top)
        full = jnp.sum(share * part, axis=0) / jnp.sum(share, axis=0)
        high = full.astype(bf16)
        out_ref[h] = high
        low = (full - high.astype(f32)).astype(bf16)
        sent = jnp.concatenate([high[None], low[None], values_ref[h]], 0)
        spread_ref[16 * h : 16 * h + 16] = jnp.broadcast_to(sent[None], (16,) + sent.shape)


def combine(parts, kept_values):
    return call(
        combine_kernel,
        "combine",
        (
            shape((heads_here, group, width), bf16),
            shape((count_rows, 6, group, width), bf16),
        ),
        cost_estimate=pl.CostEstimate(
            flops=2 * 2**20, bytes_accessed=2 * 2**20, transcendentals=2048
        ),
    )(parts, kept_values)


def reciprocal(x):
    r = pltpu.reciprocal(x, approx=True)
    return r * (2.0 - x * r)


def eliminate(w, o, size):
    p, q, s = w[o, o], w[o, o + 1], w[o + 1, o + 1]
    r = reciprocal(p * s - q * q)
    side = range(o + 2, size)
    turned = {u: (s * w[o, u] - q * w[o + 1, u], p * w[o + 1, u] - q * w[o, u]) for u in side}
    left = {}
    for u in side:
        for v in range(u, size):
            left[u, v] = w[u, v] - (w[o, u] * turned[v][0] + w[o + 1, u] * turned[v][1]) * r
    return left, turned, (s * r, -q * r, p * r), r


def invert_block(a, n, h):
    b = 4
    lane = lax.broadcasted_iota(jnp.int32, (8, n), 1)
    sub = lax.broadcasted_iota(jnp.int32, (8, n), 0)
    lane_n = lax.broadcasted_iota(jnp.int32, (n, n), 1)

    def over(v, r):
        return jnp.broadcast_to(v[r % 8 : r % 8 + 1, :], (8, n))

    for first in range(0, n, h):
        tiles = [a[first + 8 * i : first + 8 * i + 8, :] for i in range(h // 8)]
        d = None
        for k in range(first, first + h, b):
            at, off = (k - first) // 8, k % 8
            last = k + b >= first + h
            columns = [
                [jnp.broadcast_to(tile[:, k + s : k + s + 1], (8, n)) for tile in tiles]
                for s in range(b)
            ]
            if d is None:
                d = {(s, t): over(columns[s][at], k + t) for s in range(b) for t in range(s, b)}
            w = dict(d)
            if not last:
                then = (k + b - first) // 8
                for s in range(b):
                    for t in range(b):
                        w[s, b + t] = over(columns[s][then], k + b + t)
                    ahead = jnp.broadcast_to(
                        tiles[then][:, k + b + s : k + b + s + 1], (8, n)
                    )
                    for t in range(s, b):
                        w[b + s, b + t] = over(ahead, k + b + t)
            inside = (lane >= k) & (lane < k + b)
            rows = [
                jnp.where(lane == k + s, 1.0, jnp.where(inside, 0.0, over(tiles[at], off + s)))
                for s in range(b)
            ]
            size = b if last else 2 * b
            w1, turned, (i00, i01, i11), r1 = eliminate(w, 0, size)
            w2, _, (j00, j01, j11), _ = eliminate(w1, 2, size)
            n0 = i00 * rows[0] + i01 * rows[1]
            n1 = i01 * rows[0] + i11 * rows[1]
            m2 = rows[2] - (w[0, 2] * n0 + w[1, 2] * n1)
            m3 = rows[3] - (w[0, 3] * n0 + w[1, 3] * n1)
            n2 = j00 * m2 + j01 * m3
            n3 = j01 * m2 + j11 * m3
            n0 = n0 - (turned[2][0] * r1 * n2 + turned[3][0] * r1 * n3)
            n1 = n1 - (turned[2][1] * r1 * n2 + turned[3][1] * r1 * n3)
            new = [n0, n1, n2, n3]
            if not last:
                d = {(s, t): w2[b + s, b + t] for s in range(b) for t in range(s, b)}
            after = []
            for i, tile in enumerate(tiles):
                c = [columns[s][i] for s in range(b)]
                left = jnp.where(inside, 0.0, tile) - (
                    (c[0] * n0 + c[1] * n1) + (c[2] * n2 + c[3] * n3)
                )
                if i == at:
                    for s in range(b):
                        left = jnp.where(sub == off + s, new[s], left)
                after.append(left)
            tiles = after
        r = jnp.concatenate(tiles, 0)
        inside_n = (lane_n >= first) & (lane_n < first + h)
        rest = jnp.where(inside_n, 0.0, a) - jnp.dot(
            a[:, first : first + h], r, precision=highest, preferred_element_type=f32
        )
        pieces = ([rest[:first]] if first else []) + [r]
        a = jnp.concatenate(pieces + ([rest[first + h :]] if first + h < n else []), 0)
    return a


def block_steps(a, d, left, r, first, stop):
    n = 128
    row = lax.broadcasted_iota(jnp.int32, (n, n), 0)
    column = lax.broadcasted_iota(jnp.int32, (n, n), 1)
    eye = jnp.where(row == column, 1.0, 0.0)

    def step(k, _):
        at = pl.ds(pl.multiple_of(k * n, n), n)
        then = pl.ds(pl.multiple_of(jnp.minimum(k + 1, kept // n - 1) * n, n), n)
        a[...] -= jnp.dot(left[...], r[...], precision=highest, preferred_element_type=f32)
        p = invert_block(d[...], n, panel)
        a[at, at] = -eye
        left[...] = a[:, at]
        a[:, at] = jnp.zeros((kept, n), f32)
        a[at, at] = eye
        r[...] = jnp.dot(p, a[at, :], precision=highest, preferred_element_type=f32)
        a[at, :] = jnp.zeros((n, kept), f32)
        d[...] = a[then, then] - jnp.dot(
            left[then, :], r[:, then], precision=highest, preferred_element_type=f32
        )
        return 0

    lax.fori_loop(first, stop, step, 0)


def gram_kernel(flag_ref, index_ref, packets_ref, dense_ref, slot_ref, mixing, a, d, left, r, keys):
    head = spread_index()[0]
    index = index_ref[pl.ds(head, 1), :]
    holder = jnp.broadcast_to(index >> 11, (width, kept))
    down = holder.T
    row = lax.broadcasted_iota(jnp.int32, (kept, width), 0)
    lane = lax.broadcasted_iota(jnp.int32, (kept, width), 1)
    same = jnp.zeros((kept, width), f32)
    for g in range(kept // width):
        across = holder[:1, g * width : (g + 1) * width]
        same += jnp.where((down == across) & (lane + g * width < row), 1.0, 0.0)
    rank = jnp.sum(same, axis=1, keepdims=True)
    slot_ref[...] = (down * slots).astype(f32) + rank
    sent = packets_ref[:, heads_here:].astype(f32).reshape(count_rows * slots, width).astype(bf16)
    keys[...] = jnp.dot(
        one_hot(slot_ref[...], count_rows * slots), sent, preferred_element_type=f32
    ).astype(bf16)

    @pl.when(flag_ref[0] > 0)
    def _():
        keys[...] = dense_ref[:, :width]

    q = packets_ref[:, head].astype(f32).reshape(count_rows * group, width).astype(bf16)
    s = lax.dot_general(
        keys[...], q, (((1,), (1,)), ((), ())), preferred_element_type=f32
    )
    e = jnp.exp((s - jnp.max(s, axis=0, keepdims=True)) * scale)
    mixing[...] = e / jnp.sum(e, axis=0, keepdims=True)
    row = lax.broadcasted_iota(jnp.int32, (kept, kept), 0)
    column = lax.broadcasted_iota(jnp.int32, (kept, kept), 1)
    a[...] = lax.dot_general(
        mixing[...],
        mixing[...],
        (((1,), (1,)), ((), ())),
        precision=highest,
        preferred_element_type=f32,
    ) + jnp.where(row == column, ridge_weight, 0.0)
    n = 128
    d[...] = a[:n, :n]
    left[...] = jnp.zeros(left.shape, f32)
    r[...] = jnp.zeros(r.shape, f32)
    if early:
        block_steps(a, d, left, r, 0, early)


def gram(flag, kept_index, packets, dense):
    n = 128
    return call(
        gram_kernel,
        "gram",
        (
            shape((kept, width), f32),
            shape((kept, kept), f32),
            shape((kept, kept), f32),
            shape((n, n), f32),
            shape((kept, n), f32),
            shape((n, kept), f32),
        ),
        in_specs=[whole_smem] + [whole_vmem] * 3,
        out_specs=tuple([whole_vmem] * 6),
        scratch_shapes=[pltpu.VMEM((kept, width), bf16)],
        cost_estimate=pl.CostEstimate(
            flops=10**10, bytes_accessed=6 * 2**20, transcendentals=2**18
        ),
    )(flag, kept_index, packets, dense)


def in_pieces(x):
    high = x.astype(bf16)
    rest = x - high.astype(f32)
    middle = rest.astype(bf16)
    low = (rest - middle.astype(f32)).astype(bf16)
    return jnp.concatenate([high, middle, low], 0)


def weigh_kernel(
    flag_ref, slot_ref, mixing, a_ref, d_ref, left_ref, r_ref, dense_ref,
    weight_ref, share_ref, plain_ref, a, d, left, r,
):
    a[...] = a_ref[...]
    d[...] = d_ref[...]
    left[...] = left_ref[...]
    r[...] = r_ref[...]
    own = spread_index()[1]
    block_steps(a, d, left, r, early, 4)
    rows = [pl.ds(pl.multiple_of(128 * i + 8 * own, 8), 8) for i in range(4)]
    picked = jnp.concatenate([a[at, :] for at in rows], 0)
    picked -= jnp.dot(
        jnp.concatenate([left[at, :] for at in rows], 0),
        r[...],
        precision=highest,
        preferred_element_type=f32,
    )
    weight_ref[...] = in_pieces(
        jnp.dot(picked, mixing[...], precision=highest, preferred_element_type=f32)
    )

    @pl.when(flag_ref[0] == 0)
    def _():
        hot = one_hot(slot_ref[...], count_rows * slots)
        share_ref[...] = jnp.dot(
            in_pieces(ridge_weight * picked), hot, preferred_element_type=f32
        ).astype(bf16)
        plain_ref[...] = jnp.zeros(plain_ref.shape, f32)

    @pl.when(flag_ref[0] > 0)
    def _():
        share_ref[...] = jnp.zeros(share_ref.shape, bf16)
        plain_ref[...] = jnp.dot(
            ridge_weight * picked,
            dense_ref[:, width:].astype(f32),
            precision=highest,
            preferred_element_type=f32,
        )


def weigh(flag, slot, mixing, a, d, left, r, dense):
    n = 128
    return call(
        weigh_kernel,
        "weigh",
        (
            shape((96, kept), bf16),
            shape((96, count_rows * slots), bf16),
            shape((32, width), f32),
        ),
        in_specs=[whole_smem] + [whole_vmem] * 7,
        scratch_shapes=[
            pltpu.VMEM((kept, kept), f32),
            pltpu.VMEM((n, n), f32),
            pltpu.VMEM((kept, n), f32),
            pltpu.VMEM((n, kept), f32),
        ],
        cost_estimate=pl.CostEstimate(
            flops=2 * 10**10, bytes_accessed=6 * 2**20, transcendentals=0
        ),
    )(flag, slot, mixing, a, d, left, r, dense)


def finish_kernel(weight_ref, share_ref, plain_ref, sent_ref, out_ref):
    sent = sent_ref[...].astype(f32)
    targets = jnp.concatenate(
        [sent[:, i].reshape(count_rows * group, width) for i in range(2)], 1
    ).astype(bf16)
    values = sent[:, 2:].reshape(count_rows * slots, width).astype(bf16)
    fitted = jnp.dot(weight_ref[...], targets, preferred_element_type=f32)
    shared = jnp.dot(share_ref[...], values, preferred_element_type=f32)
    total = fitted[:, :width] + fitted[:, width:] + shared
    total = total[:32] + total[32:64] + total[64:] + plain_ref[...]
    out_ref[...] = total.reshape(4, 8, width)


def finish(weight, share, plain, sent):
    return call(
        finish_kernel,
        "finish",
        shape((4, 8, width), f32),
        cost_estimate=pl.CostEstimate(
            flops=2 * 96 * 2560 * 256, bytes_accessed=2**20, transcendentals=0
        ),
    )(weight, share, plain, sent)


def dense_rows(kept_index, cache_keys, cache_values):
    local_index = kept_index - own_base()
    inside = (local_index >= 0) & (local_index < local_len)
    at = jnp.clip(local_index, 0, local_len - 1)
    head = jnp.arange(heads_here, dtype=jnp.int32)[:, None]
    rows = jnp.concatenate([cache_keys[at, head], cache_values[at, head]], -1)
    rows = jnp.where(inside[..., None], rows, 0).reshape(count_rows, 32, 2 * width)
    parts = lax.all_to_all(rows, seq_axes, 0, 0)
    found = jnp.sum(parts.astype(f32), axis=0).astype(bf16)
    found = jnp.broadcast_to(found[None], (16,) + found.shape)
    return lax.all_to_all(found, ("y", "z"), 0, 0).reshape(kept, 2 * width)


def on_device(ref_queries, query_pos, cache_keys, cache_values, kept_index):
    keys = cache_keys.reshape(local_len * heads_here, width)
    values = cache_values.reshape(local_len * heads_here, width)
    packets, slot = pack(
        query_pos, kept_index, ref_queries.reshape(heads_here, group, width), keys
    )
    packets = lax.all_to_all(packets, seq_axes, 0, 0)
    both, kept_values = regroup(slot, keys, values)
    crowded = jnp.max(packets[:, 7, 7, 3].astype(f32)) > 0.0
    dense = lax.cond(
        crowded,
        dense_rows,
        lambda *_: jnp.zeros((kept, 2 * width), bf16),
        kept_index,
        cache_keys,
        cache_values,
    )
    flag = crowded.astype(jnp.int32)[None]

    parts = lax.all_to_all(attend(packets, both), seq_axes, 0, 0)
    state = gram(flag, kept_index, packets, dense)
    out, sent = combine(parts, kept_values)
    sent = lax.all_to_all(sent, seq_axes, 0, 0)
    fitted = finish(*weigh(flag, *state, dense), sent)
    fitted = lax.all_to_all(fitted, "x", 0, 0)
    return (out.reshape(1, heads_here * group, width), fitted)


def solution(mesh):
    split = Mesh(mesh.devices.reshape(4, 4, 4, 2), seq_axes + ("head",))
    in_specs = (
        P(seq_axes, "head", None),
        P(seq_axes),
        P(seq_axes, "head", None),
        P(seq_axes, "head", None),
        P("head", None),
    )
    out_specs = (P(seq_axes, "head", None), P("head", seq_axes, None))
    return jax.shard_map(
        on_device, mesh=split, in_specs=in_specs, out_specs=out_specs, check_vma=False
    )
```

```python
import functools
import math

import jax
import jax.numpy as jnp
from jax import lax
from jax.experimental import pallas as pl
from jax.experimental.pallas import tpu as pltpu
from jax.sharding import Mesh, PartitionSpec as P

ridge_weight = 0.01
masked_score = -1e30
highest = lax.Precision.HIGHEST
f32 = jnp.float32
bf16 = jnp.bfloat16

seq_axes = ("x", "y", "z")
count_rows = 64
heads_here = 4
group = 8
width = 128
local_len = 2048
kept = 512
chunk = 512
slots = 24
slot_tiles = slots // 8
panel = 64
early = 1
scale = width ** (-0.5)
scale_log2 = scale * math.log2(math.e)


def params(mib):
    return pltpu.CompilerParams(vmem_limit_bytes=mib * 2**20)


def call(kernel, name, out_shape, **more):
    return pl.pallas_call(kernel, name=name, out_shape=out_shape, **more)


def shape(dims, dtype):
    return jax.ShapeDtypeStruct(dims, dtype)


whole_vmem = pl.BlockSpec(memory_space=pltpu.VMEM)
whole_smem = pl.BlockSpec(memory_space=pltpu.SMEM)
whole_any = pl.BlockSpec(memory_space=pl.ANY)
whole_hbm = pl.BlockSpec(memory_space=pltpu.HBM)


def spread_index():
    at = [lax.axis_index(name) for name in seq_axes]
    return at[0], at[1] * 4 + at[2]


def own_base():
    plane, own = spread_index()
    return (plane * 16 + own) * local_len


def pack_kernel(
    pos_ref, index_ref, queries_ref, keys_ref, values_ref, packet_ref, *refs
):
    later_refs, (slot, found, crowd) = refs[:4], refs[4:]
    step = pl.program_id(0)
    rows = chunk * heads_here

    @pl.when(step == 0)
    def _():
        local = index_ref[...] - own_base()
        inside = (local >= 0) & (local < local_len)
        row_id = lax.broadcasted_iota(jnp.int32, (kept, kept), 0)
        lane_id = lax.broadcasted_iota(jnp.int32, (kept, kept), 1)
        before = jnp.where(row_id < lane_id, 1.0, 0.0).astype(bf16)
        rank = jnp.dot(
            jnp.where(inside, 1.0, 0.0).astype(bf16), before, preferred_element_type=f32
        )
        rank = jnp.where(inside, rank, -1.0)
        most = jnp.max(jnp.max(rank, axis=1, keepdims=True), axis=0, keepdims=True)
        crowd[...] = jnp.broadcast_to(jnp.where(most >= slots - 1.0, 1.0, 0.0), crowd.shape)
        spot = (local * heads_here + 1).astype(f32)
        slot_id = lax.broadcasted_iota(jnp.int32, (slots, kept), 0).astype(f32)
        for h in range(heads_here):
            mine = jnp.where(rank[h : h + 1] == slot_id, spot[h : h + 1] + float(h), 0.0)
            taken = jnp.sum(mine, axis=1, keepdims=True) - 1.0
            slot[h * slots : (h + 1) * slots] = jnp.broadcast_to(taken, (slots, width))
        found[...] = jnp.zeros(found.shape, f32)

    found[...] += jnp.dot(
        one_hot(slot[...] - (step * rows).astype(f32), rows),
        jnp.concatenate([keys_ref[...], values_ref[...]], 1),
        preferred_element_type=f32,
    )

    @pl.when(step == local_len // chunk - 1)
    def _():
        at = pos_ref[0]
        sub = lax.broadcasted_iota(jnp.int32, (group, width), 0)
        lane = lax.broadcasted_iota(jnp.int32, (group, width), 1)
        pieces = jnp.where(
            lane == 0, at & 255, jnp.where(lane == 1, (at >> 8) & 255, at >> 16)
        ).astype(f32)
        pieces = jnp.where(lane == 3, crowd[...], pieces)
        for h in range(heads_here):
            sent = found[h * slots : (h + 1) * slots, :width].reshape(slot_tiles, 8, width)
            last = jnp.where(sub == 7, pieces, sent[slot_tiles - 1])
            full = jnp.concatenate(
                [queries_ref[...].astype(f32), sent[: slot_tiles - 1], last[None]], 0
            ).astype(bf16)
            packet_ref[16 * h : 16 * h + 16] = jnp.broadcast_to(full[None], (16,) + full.shape)
        plane = spread_index()[0]
        for k, later_ref in enumerate(later_refs):
            own = pl.ds(pl.multiple_of((plane ^ k) * slots, 8), slots)
            later_ref[...] = found[own, width:].reshape(slot_tiles, 8, width).astype(bf16)


def one_hot(wanted, size):
    lane = lax.broadcasted_iota(jnp.int32, wanted.shape, 1).astype(wanted.dtype)
    return jnp.concatenate(
        [
            jnp.where(wanted == lane + g * width, 1.0, 0.0).astype(bf16)
            for g in range(size // width)
        ],
        1,
    )


def pack(query_pos, kept_index, queries, keys, values):
    rows = chunk * heads_here
    return call(
        pack_kernel,
        "pack",
        (
            shape((count_rows, heads_here + slot_tiles, 8, width), bf16),
        )
        + (shape((slot_tiles, 8, width), bf16),) * 4,
        grid=(local_len // chunk,),
        in_specs=[
            whole_smem,
            pl.BlockSpec((heads_here, kept), lambda i: (0, 0)),
            pl.BlockSpec((heads_here, group, width), lambda i: (0, 0, 0)),
            pl.BlockSpec((rows, width), lambda i: (i, 0)),
            pl.BlockSpec((rows, width), lambda i: (i, 0)),
        ],
        out_specs=[
            pl.BlockSpec(
                (count_rows, heads_here + slot_tiles, 8, width), lambda i: (0, 0, 0, 0)
            ),
        ]
        + [pl.BlockSpec((slot_tiles, 8, width), lambda i: (0, 0, 0))] * 4,
        scratch_shapes=[
            pltpu.VMEM((heads_here * slots, width), f32),
            pltpu.VMEM((heads_here * slots, 2 * width), f32),
            pltpu.VMEM((group, width), f32),
        ],
        cost_estimate=pl.CostEstimate(
            flops=2 * 128 * 8192 * 256, bytes_accessed=5 * 2**20, transcendentals=0
        ),
        compiler_params=params(60),
    )(query_pos, kept_index, queries, keys, values)


def attend_kernel(
    queries_ref, keys_ref, values_ref, packet_ref, flag_ref, raw, wide, keys, values, side, sem
):
    move = pltpu.make_async_copy(values_ref, raw, sem)
    move.start()
    tile = 256
    parts = count_rows * group // tile
    wide[0] = keys_ref[...].astype(f32)
    lane = lax.broadcasted_iota(jnp.int32, (local_len, width), 1)
    lane_t = lax.broadcasted_iota(jnp.int32, (tile, width), 1)
    row_t = lax.broadcasted_iota(jnp.int32, (tile, width), 0)
    pieces = queries_ref[:, heads_here + slot_tiles - 1].astype(f32)[:, 7]
    flag_ref[0] = (jnp.max(pieces[:, 3:4]) > 0.0).astype(jnp.int32)
    row_id = lax.broadcasted_iota(jnp.int32, (count_rows, width), 0)
    lane_id = lax.broadcasted_iota(jnp.int32, (count_rows, width), 1)
    place = pieces[:, 0:1] + 256.0 * pieces[:, 1:2] + 65536.0 * pieces[:, 2:3]
    place = jnp.sum(jnp.where(row_id == lane_id, place, 0.0), axis=0, keepdims=True)
    spot = lax.broadcasted_iota(jnp.int32, (local_len, width), 0) + own_base()
    late = (spot.astype(f32) > place) & (lane < count_rows)
    late = jnp.where(late, masked_score, 0.0).astype(bf16)
    ones = jnp.where(lane == 0, 1.0, 0.0).astype(bf16)
    for i in range(2):
        keys[i, :, width:] = late
        values[i, :, width:] = ones
    side[...] = jnp.zeros(side.shape, f32)

    def scores(h, part):
        at = pl.ds(h, local_len, stride=heads_here)
        if part == 0:
            keys[h % 2, :, :width] = wide[0, at, :].astype(bf16)
            if h == 0:
                move.wait()
                wide[1] = raw[...].astype(f32)
            values[h % 2, :, :width] = wide[1, at, :].astype(bf16)
        rows = tile // group
        q = queries_ref[part * rows : (part + 1) * rows, h].astype(f32).reshape(tile, width)
        own = jnp.where(row_t // group + part * rows == lane_t, 1.0, 0.0)
        q = jnp.concatenate([q, own], 1).astype(bf16)
        return lax.dot_general(
            q, keys[h % 2], (((1,), (1,)), ((), ())), preferred_element_type=f32
        )

    steps = [(h, part) for h in range(heads_here) for part in range(parts)]
    s = scores(*steps[0])
    for i, (h, part) in enumerate(steps):
        after = scores(*steps[i + 1]) if i + 1 < len(steps) else None
        peak = jnp.max(s, axis=1, keepdims=True)
        w = jnp.exp2((s - peak) * scale_log2).astype(bf16)
        o = jnp.dot(w, values[h % 2], preferred_element_type=f32)
        sums = o[:, width : width + 1]
        mass = peak * scale_log2 + jnp.log2(sums)
        high = mass.astype(bf16).astype(f32)
        middle = (mass - high).astype(bf16).astype(f32)
        low = mass - high - middle
        first = 3 * (row_t // 128 + part * 2)
        mark = jnp.where(
            lane_t == first,
            high,
            jnp.where(lane_t == first + 1, middle, jnp.where(lane_t == first + 2, low, 0.0)),
        )
        to = slice(16 * h, 16 * h + 16)
        mark = mark.reshape(2, 16, group, width)
        done = (o[:, :width] / sums).reshape(2, 16, group, width).astype(bf16)
        for x in range(2):
            packet_ref[to, 2 * part + x] = done[x]
        side[to] += mark[0] + mark[1]
        s = after
    packet_ref[:, 4] = side[...].astype(bf16)


def attend(packets, keys, values):
    return call(
        attend_kernel,
        "attend",
        (
            shape((count_rows, heads_here + 1, group, width), bf16),
            shape((1,), jnp.int32),
        ),
        in_specs=[whole_vmem] * 2 + [whole_hbm],
        out_specs=[whole_vmem, whole_smem],
        scratch_shapes=[
            pltpu.VMEM((local_len * heads_here, width), bf16),
            pltpu.VMEM((2, local_len * heads_here, width), f32),
            pltpu.VMEM((2, local_len, 2 * width), bf16),
            pltpu.VMEM((2, local_len, 2 * width), bf16),
            pltpu.VMEM((count_rows, group, width), f32),
            pltpu.SemaphoreType.DMA,
        ],
        cost_estimate=pl.CostEstimate(
            flops=2 * 2 * 512 * 2048 * 256 * 4,
            bytes_accessed=6 * 2**20,
            transcendentals=4 * 512 * 2048,
        ),
        compiler_params=params(36),
    )(packets, keys, values)


def combine_kernel(parts_ref, v0_ref, v1_ref, v2_ref, v3_ref, full_ref, spread_ref):
    side = parts_ref[:, 4].astype(f32)
    lane = lax.broadcasted_iota(jnp.int32, side.shape, 2)
    for i in range(4):
        part = parts_ref[:, i].astype(f32)
        own = (lane >= 3 * i) & (lane < 3 * i + 3)
        mass = jnp.sum(jnp.where(own, side, 0.0), axis=2, keepdims=True)
        top = jnp.max(mass, axis=0, keepdims=True)
        share = jnp.exp2(mass - top)
        full = jnp.sum(share * part, axis=0) / jnp.sum(share, axis=0)
        full_ref[i] = full
        high = full.astype(bf16)
        low = (full - high.astype(f32)).astype(bf16)
        spread_ref[:, i] = jnp.broadcast_to(high[None], (16, group, width))
        spread_ref[:, 4 + i] = jnp.broadcast_to(low[None], (16, group, width))
    for k, ref in enumerate((v0_ref, v1_ref, v2_ref, v3_ref)):
        at = 8 + k * slot_tiles
        spread_ref[:, at : at + slot_tiles] = jnp.broadcast_to(
            ref[...][None], (16, slot_tiles, 8, width)
        )


def combine(parts, kept_values):
    return call(
        combine_kernel,
        "combine",
        (
            shape((4, group, width), f32),
            shape((16, 8 + 4 * slot_tiles, group, width), bf16),
        ),
        in_specs=[whole_vmem] * 5,
        out_specs=[whole_vmem] * 2,
        cost_estimate=pl.CostEstimate(
            flops=2 * 2**20, bytes_accessed=2 * 2**20, transcendentals=2048
        ),
        compiler_params=params(12),
    )(parts, *kept_values)


def reciprocal(x):
    r = pltpu.reciprocal(x, approx=True)
    return r * (2.0 - x * r)


def eliminate(w, o, size):
    p, q, s = w[o, o], w[o, o + 1], w[o + 1, o + 1]
    r = reciprocal(p * s - q * q)
    side = range(o + 2, size)
    turned = {u: (s * w[o, u] - q * w[o + 1, u], p * w[o + 1, u] - q * w[o, u]) for u in side}
    left = {}
    for u in side:
        for v in range(u, size):
            left[u, v] = w[u, v] - (w[o, u] * turned[v][0] + w[o + 1, u] * turned[v][1]) * r
    return left, turned, (s * r, -q * r, p * r), r


def invert_block(a, n, h):
    b = 4
    lane = lax.broadcasted_iota(jnp.int32, (8, n), 1)
    sub = lax.broadcasted_iota(jnp.int32, (8, n), 0)
    lane_n = lax.broadcasted_iota(jnp.int32, (n, n), 1)

    def over(v, r):
        return jnp.broadcast_to(v[r % 8 : r % 8 + 1, :], (8, n))

    for first in range(0, n, h):
        tiles = [a[first + 8 * i : first + 8 * i + 8, :] for i in range(h // 8)]
        d = None
        for k in range(first, first + h, b):
            at, off = (k - first) // 8, k % 8
            last = k + b >= first + h
            columns = [
                [jnp.broadcast_to(tile[:, k + s : k + s + 1], (8, n)) for tile in tiles]
                for s in range(b)
            ]
            if d is None:
                d = {(s, t): over(columns[s][at], k + t) for s in range(b) for t in range(s, b)}
            w = dict(d)
            if not last:
                then = (k + b - first) // 8
                for s in range(b):
                    for t in range(b):
                        w[s, b + t] = over(columns[s][then], k + b + t)
                    ahead = jnp.broadcast_to(
                        tiles[then][:, k + b + s : k + b + s + 1], (8, n)
                    )
                    for t in range(s, b):
                        w[b + s, b + t] = over(ahead, k + b + t)
            inside = (lane >= k) & (lane < k + b)
            rows = [
                jnp.where(lane == k + s, 1.0, jnp.where(inside, 0.0, over(tiles[at], off + s)))
                for s in range(b)
            ]
            size = b if last else 2 * b
            w1, turned, (i00, i01, i11), r1 = eliminate(w, 0, size)
            w2, _, (j00, j01, j11), _ = eliminate(w1, 2, size)
            n0 = i00 * rows[0] + i01 * rows[1]
            n1 = i01 * rows[0] + i11 * rows[1]
            m2 = rows[2] - (w[0, 2] * n0 + w[1, 2] * n1)
            m3 = rows[3] - (w[0, 3] * n0 + w[1, 3] * n1)
            n2 = j00 * m2 + j01 * m3
            n3 = j01 * m2 + j11 * m3
            n0 = n0 - (turned[2][0] * r1 * n2 + turned[3][0] * r1 * n3)
            n1 = n1 - (turned[2][1] * r1 * n2 + turned[3][1] * r1 * n3)
            new = [n0, n1, n2, n3]
            if not last:
                d = {(s, t): w2[b + s, b + t] for s in range(b) for t in range(s, b)}
            after = []
            for i, tile in enumerate(tiles):
                c = [columns[s][i] for s in range(b)]
                left = jnp.where(inside, 0.0, tile) - (
                    (c[0] * n0 + c[1] * n1) + (c[2] * n2 + c[3] * n3)
                )
                if i == at:
                    for s in range(b):
                        left = jnp.where(sub == off + s, new[s], left)
                after.append(left)
            tiles = after
        r = jnp.concatenate(tiles, 0)
        inside_n = (lane_n >= first) & (lane_n < first + h)
        rest = jnp.where(inside_n, 0.0, a) - jnp.dot(
            a[:, first : first + h], r, precision=highest, preferred_element_type=f32
        )
        pieces = ([rest[:first]] if first else []) + [r]
        a = jnp.concatenate(pieces + ([rest[first + h :]] if first + h < n else []), 0)
    return a


def block_steps(a, d, left, r, first, stop):
    n = 128
    row = lax.broadcasted_iota(jnp.int32, (n, n), 0)
    column = lax.broadcasted_iota(jnp.int32, (n, n), 1)
    eye = jnp.where(row == column, 1.0, 0.0)

    def step(k, _):
        at = pl.ds(pl.multiple_of(k * n, n), n)
        then = pl.ds(pl.multiple_of(jnp.minimum(k + 1, kept // n - 1) * n, n), n)
        a[...] -= jnp.dot(left[...], r[...], precision=highest, preferred_element_type=f32)
        p = invert_block(d[...], n, panel)
        a[at, at] = -eye
        left[...] = a[:, at]
        a[:, at] = jnp.zeros((kept, n), f32)
        a[at, at] = eye
        r[...] = jnp.dot(p, a[at, :], precision=highest, preferred_element_type=f32)
        a[at, :] = jnp.zeros((n, kept), f32)
        d[...] = a[then, then] - jnp.dot(
            left[then, :], r[:, then], precision=highest, preferred_element_type=f32
        )
        return 0

    lax.fori_loop(first, stop, step, 0)


def gram_kernel(
    flag_ref, index_ref, packets_ref, dense_ref,
    slot_ref, mixing_ref, a, d, left, r, keys, dense, slot, mixing, sems,
):
    head = spread_index()[0]
    index = index_ref[pl.ds(head, 1), :]
    holder = jnp.broadcast_to(index >> 11, (width, kept))
    down = holder.T
    row = lax.broadcasted_iota(jnp.int32, (kept, width), 0)
    lane = lax.broadcasted_iota(jnp.int32, (kept, width), 1)
    same = jnp.zeros((kept, width), f32)
    for g in range(kept // width):
        across = holder[:1, g * width : (g + 1) * width]
        same += jnp.where((down == across) & (lane + g * width < row), 1.0, 0.0)
    rank = jnp.sum(same, axis=1, keepdims=True)
    own = (down & 15) * 4 + ((down >> 4) ^ head)
    slot[...] = (own * slots).astype(f32) + rank
    slot_out = pltpu.make_async_copy(slot, slot_ref, sems.at[0])
    slot_out.start()
    sent = packets_ref[:, heads_here:].astype(f32).reshape(count_rows * slots, width).astype(bf16)
    keys[...] = jnp.dot(
        one_hot((down * slots).astype(f32) + rank, count_rows * slots),
        sent,
        preferred_element_type=f32,
    ).astype(bf16)

    @pl.when(flag_ref[0] > 0)
    def _():
        slot_out.wait()
        pltpu.sync_copy(dense_ref, dense)
        keys[...] = dense[:, :width]
        slot[...] = dense[:, width:].astype(f32)
        slot_out.start()

    q = packets_ref[:, head].astype(f32).reshape(count_rows * group, width).astype(bf16)
    s = lax.dot_general(
        keys[...], q, (((1,), (1,)), ((), ())), preferred_element_type=f32
    )
    e = jnp.exp((s - jnp.max(s, axis=0, keepdims=True)) * scale)
    mixing[...] = e / jnp.sum(e, axis=0, keepdims=True)
    mixing_out = pltpu.make_async_copy(mixing, mixing_ref, sems.at[1])
    mixing_out.start()
    row = lax.broadcasted_iota(jnp.int32, (kept, kept), 0)
    column = lax.broadcasted_iota(jnp.int32, (kept, kept), 1)
    a[...] = lax.dot_general(
        mixing[...],
        mixing[...],
        (((1,), (1,)), ((), ())),
        precision=highest,
        preferred_element_type=f32,
    ) + jnp.where(row == column, ridge_weight, 0.0)
    n = 128
    d[...] = a[:n, :n]
    left[...] = jnp.zeros(left.shape, f32)
    r[...] = jnp.zeros(r.shape, f32)
    block_steps(a, d, left, r, 0, early)
    slot_out.wait()
    mixing_out.wait()


def gram(flag, kept_index, packets, dense):
    n = 128
    return call(
        gram_kernel,
        "gram",
        (
            shape((kept, width), f32),
            shape((kept, kept), f32),
            shape((kept, kept), f32),
            shape((n, n), f32),
            shape((kept, n), f32),
            shape((n, kept), f32),
        ),
        in_specs=[whole_smem] + [whole_vmem] * 2 + [whole_any],
        out_specs=[whole_any] * 2 + [whole_vmem] * 4,
        scratch_shapes=[
            pltpu.VMEM((kept, width), bf16),
            pltpu.VMEM((kept, 2 * width), bf16),
            pltpu.VMEM((kept, width), f32),
            pltpu.VMEM((kept, kept), f32),
            pltpu.SemaphoreType.DMA((2,)),
        ],
        cost_estimate=pl.CostEstimate(
            flops=10**10, bytes_accessed=6 * 2**20, transcendentals=2**18
        ),
        compiler_params=params(24),
    )(flag, kept_index, packets, dense)


def in_pieces(x):
    high = x.astype(bf16)
    rest = x - high.astype(f32)
    middle = rest.astype(bf16)
    low = (rest - middle.astype(f32)).astype(bf16)
    return jnp.concatenate([high, middle, low], 0)


def weigh_kernel(
    flag_ref, slot_ref, mixing_ref, a_ref, d_ref, left_ref, r_ref,
    weight_ref, share_ref, plain_ref, a, d, left, r, slot, mixing, sems,
):
    slot_in = pltpu.make_async_copy(slot_ref, slot, sems.at[0])
    mixing_in = pltpu.make_async_copy(mixing_ref, mixing, sems.at[1])
    slot_in.start()
    mixing_in.start()
    a[...] = a_ref[...]
    d[...] = d_ref[...]
    left[...] = left_ref[...]
    r[...] = r_ref[...]
    plane, own = spread_index()
    block_steps(a, d, left, r, early, 4)
    rows = [pl.ds(pl.multiple_of(128 * (plane ^ k) + 8 * own, 8), 8) for k in range(4)]
    picked = jnp.concatenate([a[at, :] for at in rows], 0)
    picked -= jnp.dot(
        jnp.concatenate([left[at, :] for at in rows], 0),
        r[...],
        precision=highest,
        preferred_element_type=f32,
    )
    slot_in.wait()
    mixing_in.wait()
    weight_ref[...] = in_pieces(
        jnp.dot(picked, mixing[...], precision=highest, preferred_element_type=f32)
    )

    @pl.when(flag_ref[0] == 0)
    def _():
        hot = one_hot(slot[...], count_rows * slots)
        share_ref[...] = jnp.dot(
            in_pieces(ridge_weight * picked), hot, preferred_element_type=f32
        ).astype(bf16)
        plain_ref[...] = jnp.zeros(plain_ref.shape, f32)

    @pl.when(flag_ref[0] > 0)
    def _():
        share_ref[...] = jnp.zeros(share_ref.shape, bf16)
        plain_ref[...] = jnp.dot(
            ridge_weight * picked, slot[...], precision=highest, preferred_element_type=f32
        )


def weigh(flag, slot, mixing, a, d, left, r):
    n = 128
    return call(
        weigh_kernel,
        "weigh",
        (
            shape((96, kept), bf16),
            shape((96, count_rows * slots), bf16),
            shape((32, width), f32),
        ),
        in_specs=[whole_smem] + [whole_any] * 2 + [whole_vmem] * 4,
        out_specs=[whole_vmem] * 3,
        scratch_shapes=[
            pltpu.VMEM((kept, kept), f32),
            pltpu.VMEM((n, n), f32),
            pltpu.VMEM((kept, n), f32),
            pltpu.VMEM((n, kept), f32),
            pltpu.VMEM((kept, width), f32),
            pltpu.VMEM((kept, kept), f32),
            pltpu.SemaphoreType.DMA((2,)),
        ],
        cost_estimate=pl.CostEstimate(
            flops=2 * 10**10, bytes_accessed=6 * 2**20, transcendentals=0
        ),
        compiler_params=params(20),
    )(flag, slot, mixing, a, d, left, r)


def finish_kernel(weight_ref, share_ref, plain_ref, full_ref, sent_ref, *out_refs):
    sent = sent_ref[...].astype(f32)
    targets = [
        jnp.concatenate(
            [sent[:, 4 * i + x].reshape(16 * group, width) for x in range(4)], 0
        )
        for i in range(2)
    ]
    values = sent[:, 8:].reshape(count_rows * slots, width).astype(bf16)
    fitted = jnp.dot(
        weight_ref[...], jnp.concatenate(targets, 1).astype(bf16), preferred_element_type=f32
    )
    shared = jnp.dot(share_ref[...], values, preferred_element_type=f32)
    total = fitted[:, :width] + fitted[:, width:] + shared
    total = total[:32] + total[32:64] + total[64:] + plain_ref[...]
    plane = spread_index()[0]
    for k, out_ref in enumerate(out_refs):
        out_ref[:8] = total[8 * k : 8 * k + 8]
        out_ref[8:] = full_ref[plane ^ k]


def finish(weight, share, plain, full, sent):
    return call(
        finish_kernel,
        "finish",
        [shape((16, width), f32)] * 4,
        in_specs=[whole_vmem] * 5,
        out_specs=[whole_vmem] * 4,
        cost_estimate=pl.CostEstimate(
            flops=2 * 96 * 2560 * 256, bytes_accessed=2**20, transcendentals=0
        ),
        compiler_params=params(10),
    )(weight, share, plain, full, sent)


def arrange_kernel(b0_ref, b1_ref, b2_ref, b3_ref, out_ref, fitted_ref):
    plane = spread_index()[0]
    for k, ref in enumerate((b0_ref, b1_ref, b2_ref, b3_ref)):
        fitted_ref[plane ^ k] = ref[:8]
        out_ref[plane ^ k] = ref[8:].astype(bf16)


def arrange(blocks):
    return call(
        arrange_kernel,
        "arrange",
        (shape((heads_here, group, width), bf16), shape((heads_here, 8, width), f32)),
        in_specs=[whole_vmem] * 4,
        out_specs=[whole_vmem] * 2,
        cost_estimate=pl.CostEstimate(flops=2**13, bytes_accessed=2**16, transcendentals=0),
        compiler_params=params(4),
    )(*blocks)


def dense_rows(kept_index, cache_keys, cache_values):
    local_index = kept_index - own_base()
    inside = (local_index >= 0) & (local_index < local_len)
    at = jnp.clip(local_index, 0, local_len - 1)
    head = jnp.arange(heads_here, dtype=jnp.int32)[:, None]
    rows = jnp.concatenate([cache_keys[at, head], cache_values[at, head]], -1)
    rows = jnp.where(inside[..., None], rows, 0).reshape(count_rows, 32, 2 * width)
    parts = lax.all_to_all(rows, seq_axes, 0, 0)
    found = jnp.sum(parts.astype(f32), axis=0).astype(bf16)
    found = jnp.broadcast_to(found[None], (16,) + found.shape)
    return lax.all_to_all(found, ("y", "z"), 0, 0).reshape(kept, 2 * width)


def along_x(blocks):
    return [blocks[0]] + [
        lax.ppermute(blocks[k], "x", [(i, i ^ k) for i in range(4)]) for k in range(1, 4)
    ]


def on_device(ref_queries, query_pos, cache_keys, cache_values, kept_index):
    keys = cache_keys.reshape(local_len * heads_here, width)
    values = cache_values.reshape(local_len * heads_here, width)
    packets, *kept_values = pack(
        query_pos, kept_index, ref_queries.reshape(heads_here, group, width), keys, values
    )
    packets = lax.all_to_all(packets, seq_axes, 0, 0)
    kept_values = along_x(kept_values)
    parts, flag = attend(packets, keys, values)
    parts = lax.all_to_all(parts, seq_axes, 0, 0)
    dense = lax.cond(
        flag[0] > 0,
        dense_rows,
        lambda *_: jnp.zeros((kept, 2 * width), bf16),
        kept_index,
        cache_keys,
        cache_values,
    )
    state = gram(flag, kept_index, packets, dense)
    full, sent = combine(parts, kept_values)
    sent = lax.all_to_all(sent, ("y", "z"), 0, 0)
    out, fitted = arrange(along_x(finish(*weigh(flag, *state), full, sent)))
    return (out.reshape(1, heads_here * group, width), fitted)


def solution(mesh):
    split = Mesh(mesh.devices.reshape(4, 4, 4, 2), seq_axes + ("head",))
    in_specs = (
        P(seq_axes, "head", None),
        P(seq_axes),
        P(seq_axes, "head", None),
        P(seq_axes, "head", None),
        P("head", None),
    )
    out_specs = (P(seq_axes, "head", None), P("head", seq_axes, None))
    return jax.shard_map(
        on_device, mesh=split, in_specs=in_specs, out_specs=out_specs, check_vma=False
    )
```

```python
import functools
import math

import jax
import jax.numpy as jnp
from jax import lax
from jax.experimental import pallas as pl
from jax.experimental.pallas import tpu as pltpu
from jax.sharding import Mesh, PartitionSpec as P

ridge_weight = 0.01
masked_score = -1e30
highest = lax.Precision.HIGHEST
f32 = jnp.float32
bf16 = jnp.bfloat16

seq_axes = ("x", "y", "z")
count_rows = 64
heads_here = 4
group = 8
width = 128
local_len = 2048
kept = 512
chunk = 1024
slots = 24
slot_tiles = slots // 8
panel = 64
scale = width ** (-0.5)
scale_log2 = scale * math.log2(math.e)


def params(mib):
    return pltpu.CompilerParams(vmem_limit_bytes=mib * 2**20)


def call(kernel, name, out_shape, **more):
    return pl.pallas_call(kernel, name=name, out_shape=out_shape, **more)


def shape(dims, dtype):
    return jax.ShapeDtypeStruct(dims, dtype)


whole_vmem = pl.BlockSpec(memory_space=pltpu.VMEM)
whole_smem = pl.BlockSpec(memory_space=pltpu.SMEM)
whole_any = pl.BlockSpec(memory_space=pl.ANY)
whole_hbm = pl.BlockSpec(memory_space=pltpu.HBM)


def spread_index():
    at = [lax.axis_index(name) for name in seq_axes]
    return at[0], at[1] * 4 + at[2]


def own_base():
    plane, own = spread_index()
    return (plane * 16 + own) * local_len


def pack_kernel(
    pos_ref, index_ref, queries_ref, keys_ref, values_ref, packet_ref, *refs
):
    later_refs, (slot, found, crowd) = refs[:4], refs[4:]
    step = pl.program_id(0)
    rows = chunk * heads_here

    @pl.when(step == 0)
    def _():
        local = index_ref[...] - own_base()
        inside = (local >= 0) & (local < local_len)
        row_id = lax.broadcasted_iota(jnp.int32, (kept, kept), 0)
        lane_id = lax.broadcasted_iota(jnp.int32, (kept, kept), 1)
        before = jnp.where(row_id < lane_id, 1.0, 0.0).astype(bf16)
        rank = jnp.dot(
            jnp.where(inside, 1.0, 0.0).astype(bf16), before, preferred_element_type=f32
        )
        rank = jnp.where(inside, rank, -1.0)
        most = jnp.max(jnp.max(rank, axis=1, keepdims=True), axis=0, keepdims=True)
        crowd[...] = jnp.broadcast_to(jnp.where(most >= slots - 1.0, 1.0, 0.0), crowd.shape)
        spot = (local * heads_here + 1).astype(f32)
        slot_id = lax.broadcasted_iota(jnp.int32, (slots, kept), 0).astype(f32)
        for h in range(heads_here):
            mine = jnp.where(rank[h : h + 1] == slot_id, spot[h : h + 1] + float(h), 0.0)
            taken = jnp.sum(mine, axis=1, keepdims=True) - 1.0
            slot[h * slots : (h + 1) * slots] = jnp.broadcast_to(taken, (slots, width))
        found[...] = jnp.zeros(found.shape, f32)

    found[...] += jnp.dot(
        one_hot(slot[...] - (step * rows).astype(f32), rows),
        jnp.concatenate([keys_ref[...], values_ref[...]], 1),
        preferred_element_type=f32,
    )

    @pl.when(step == local_len // chunk - 1)
    def _():
        at = pos_ref[0]
        sub = lax.broadcasted_iota(jnp.int32, (group, width), 0)
        lane = lax.broadcasted_iota(jnp.int32, (group, width), 1)
        pieces = jnp.where(
            lane == 0, at & 255, jnp.where(lane == 1, (at >> 8) & 255, at >> 16)
        ).astype(f32)
        pieces = jnp.where(lane == 3, crowd[...], pieces)
        for h in range(heads_here):
            sent = found[h * slots : (h + 1) * slots, :width].reshape(slot_tiles, 8, width)
            last = jnp.where(sub == 7, pieces, sent[slot_tiles - 1])
            full = jnp.concatenate(
                [queries_ref[...].astype(f32), sent[: slot_tiles - 1], last[None]], 0
            ).astype(bf16)
            packet_ref[16 * h : 16 * h + 16] = jnp.broadcast_to(full[None], (16,) + full.shape)
        plane = spread_index()[0]
        for k, later_ref in enumerate(later_refs):
            own = pl.ds(pl.multiple_of((plane ^ k) * slots, 8), slots)
            later_ref[...] = found[own, width:].reshape(slot_tiles, 8, width).astype(bf16)


def one_hot(wanted, size):
    lane = lax.broadcasted_iota(jnp.int32, wanted.shape, 1).astype(wanted.dtype)
    return jnp.concatenate(
        [
            jnp.where(wanted == lane + g * width, 1.0, 0.0).astype(bf16)
            for g in range(size // width)
        ],
        1,
    )


def pack(query_pos, kept_index, queries, keys, values):
    rows = chunk * heads_here
    return call(
        pack_kernel,
        "pack",
        (
            shape((count_rows, heads_here + slot_tiles, 8, width), bf16),
        )
        + (shape((slot_tiles, 8, width), bf16),) * 4,
        grid=(local_len // chunk,),
        in_specs=[
            whole_smem,
            pl.BlockSpec((heads_here, kept), lambda i: (0, 0)),
            pl.BlockSpec((heads_here, group, width), lambda i: (0, 0, 0)),
            pl.BlockSpec((rows, width), lambda i: (i, 0)),
            pl.BlockSpec((rows, width), lambda i: (i, 0)),
        ],
        out_specs=[
            pl.BlockSpec(
                (count_rows, heads_here + slot_tiles, 8, width), lambda i: (0, 0, 0, 0)
            ),
        ]
        + [pl.BlockSpec((slot_tiles, 8, width), lambda i: (0, 0, 0))] * 4,
        scratch_shapes=[
            pltpu.VMEM((heads_here * slots, width), f32),
            pltpu.VMEM((heads_here * slots, 2 * width), f32),
            pltpu.VMEM((group, width), f32),
        ],
        cost_estimate=pl.CostEstimate(
            flops=2 * 128 * 8192 * 256, bytes_accessed=5 * 2**20, transcendentals=0
        ),
        compiler_params=params(60),
    )(query_pos, kept_index, queries, keys, values)


def attend_kernel(
    queries_ref, keys_ref, values_ref, packet_ref, flag_ref, raw, wide, keys, values, side, sem
):
    move = pltpu.make_async_copy(values_ref, raw, sem)
    move.start()
    tile = 256
    parts = count_rows * group // tile
    wide[0] = keys_ref[...].astype(f32)
    lane = lax.broadcasted_iota(jnp.int32, (local_len, width), 1)
    lane_t = lax.broadcasted_iota(jnp.int32, (tile, width), 1)
    row_t = lax.broadcasted_iota(jnp.int32, (tile, width), 0)
    pieces = queries_ref[:, heads_here + slot_tiles - 1].astype(f32)[:, 7]
    flag_ref[0] = (jnp.max(pieces[:, 3:4]) > 0.0).astype(jnp.int32)
    row_id = lax.broadcasted_iota(jnp.int32, (count_rows, width), 0)
    lane_id = lax.broadcasted_iota(jnp.int32, (count_rows, width), 1)
    place = pieces[:, 0:1] + 256.0 * pieces[:, 1:2] + 65536.0 * pieces[:, 2:3]
    place = jnp.sum(jnp.where(row_id == lane_id, place, 0.0), axis=0, keepdims=True)
    spot = lax.broadcasted_iota(jnp.int32, (local_len, width), 0) + own_base()
    late = (spot.astype(f32) > place) & (lane < count_rows)
    late = jnp.where(late, masked_score, 0.0).astype(bf16)
    ones = jnp.where(lane == 0, 1.0, 0.0).astype(bf16)
    for i in range(2):
        keys[i, :, width:] = late
        values[i, :, width:] = ones
    side[...] = jnp.zeros(side.shape, f32)

    def scores(h, part):
        at = pl.ds(h, local_len, stride=heads_here)
        if part == 0:
            keys[h % 2, :, :width] = wide[0, at, :].astype(bf16)
            if h == 0:
                move.wait()
                wide[1] = raw[...].astype(f32)
            values[h % 2, :, :width] = wide[1, at, :].astype(bf16)
        rows = tile // group
        q = queries_ref[part * rows : (part + 1) * rows, h].astype(f32).reshape(tile, width)
        own = jnp.where(row_t // group + part * rows == lane_t, 1.0, 0.0)
        q = jnp.concatenate([q, own], 1).astype(bf16)
        return lax.dot_general(
            q, keys[h % 2], (((1,), (1,)), ((), ())), preferred_element_type=f32
        )

    steps = [(h, part) for h in range(heads_here) for part in range(parts)]
    s = scores(*steps[0])
    for i, (h, part) in enumerate(steps):
        after = scores(*steps[i + 1]) if i + 1 < len(steps) else None
        peak = jnp.max(s, axis=1, keepdims=True)
        w = jnp.exp2((s - peak) * scale_log2).astype(bf16)
        o = jnp.dot(w, values[h % 2], preferred_element_type=f32)
        sums = o[:, width : width + 1]
        mass = peak * scale_log2 + jnp.log2(sums)
        high = mass.astype(bf16).astype(f32)
        middle = (mass - high).astype(bf16).astype(f32)
        low = mass - high - middle
        first = 3 * (row_t // 128 + part * 2)
        mark = jnp.where(
            lane_t == first,
            high,
            jnp.where(lane_t == first + 1, middle, jnp.where(lane_t == first + 2, low, 0.0)),
        )
        to = slice(16 * h, 16 * h + 16)
        mark = mark.reshape(2, 16, group, width)
        done = (o[:, :width] / sums).reshape(2, 16, group, width).astype(bf16)
        for x in range(2):
            packet_ref[to, 2 * part + x] = done[x]
        side[to] += mark[0] + mark[1]
        s = after
    packet_ref[:, 4] = side[...].astype(bf16)


def attend(packets, keys, values):
    return call(
        attend_kernel,
        "attend",
        (
            shape((count_rows, heads_here + 1, group, width), bf16),
            shape((1,), jnp.int32),
        ),
        in_specs=[whole_vmem] * 2 + [whole_hbm],
        out_specs=[whole_vmem, whole_smem],
        scratch_shapes=[
            pltpu.VMEM((local_len * heads_here, width), bf16),
            pltpu.VMEM((2, local_len * heads_here, width), f32),
            pltpu.VMEM((2, local_len, 2 * width), bf16),
            pltpu.VMEM((2, local_len, 2 * width), bf16),
            pltpu.VMEM((count_rows, group, width), f32),
            pltpu.SemaphoreType.DMA,
        ],
        cost_estimate=pl.CostEstimate(
            flops=2 * 2 * 512 * 2048 * 256 * 4,
            bytes_accessed=6 * 2**20,
            transcendentals=4 * 512 * 2048,
        ),
        compiler_params=params(36),
    )(packets, keys, values)


def combine_kernel(parts_ref, v0_ref, v1_ref, v2_ref, v3_ref, full_ref, spread_ref):
    side = parts_ref[:, 4].astype(f32)
    lane = lax.broadcasted_iota(jnp.int32, side.shape, 2)
    for i in range(4):
        part = parts_ref[:, i].astype(f32)
        own = (lane >= 3 * i) & (lane < 3 * i + 3)
        mass = jnp.sum(jnp.where(own, side, 0.0), axis=2, keepdims=True)
        top = jnp.max(mass, axis=0, keepdims=True)
        share = jnp.exp2(mass - top)
        full = jnp.sum(share * part, axis=0) / jnp.sum(share, axis=0)
        full_ref[i] = full
        high = full.astype(bf16)
        low = (full - high.astype(f32)).astype(bf16)
        spread_ref[:, i] = jnp.broadcast_to(high[None], (16, group, width))
        spread_ref[:, 4 + i] = jnp.broadcast_to(low[None], (16, group, width))
    for k, ref in enumerate((v0_ref, v1_ref, v2_ref, v3_ref)):
        at = 8 + k * slot_tiles
        spread_ref[:, at : at + slot_tiles] = jnp.broadcast_to(
            ref[...][None], (16, slot_tiles, 8, width)
        )


def combine(parts, kept_values):
    return call(
        combine_kernel,
        "combine",
        (
            shape((4, group, width), f32),
            shape((16, 8 + 4 * slot_tiles, group, width), bf16),
        ),
        in_specs=[whole_vmem] * 5,
        out_specs=[whole_vmem] * 2,
        cost_estimate=pl.CostEstimate(
            flops=2 * 2**20, bytes_accessed=2 * 2**20, transcendentals=2048
        ),
        compiler_params=params(12),
    )(parts, *kept_values)


def reciprocal(x):
    r = pltpu.reciprocal(x, approx=True)
    return r * (2.0 - x * r)


def eliminate(w, o, size):
    p, q, s = w[o, o], w[o, o + 1], w[o + 1, o + 1]
    r = reciprocal(p * s - q * q)
    side = range(o + 2, size)
    turned = {u: (s * w[o, u] - q * w[o + 1, u], p * w[o + 1, u] - q * w[o, u]) for u in side}
    left = {}
    for u in side:
        for v in range(u, size):
            left[u, v] = w[u, v] - (w[o, u] * turned[v][0] + w[o + 1, u] * turned[v][1]) * r
    return left, turned, (s * r, -q * r, p * r), r


def invert_block(a, n, h, start, stop):
    b = 4
    lane = lax.broadcasted_iota(jnp.int32, (8, n), 1)
    sub = lax.broadcasted_iota(jnp.int32, (8, n), 0)
    lane_n = lax.broadcasted_iota(jnp.int32, (n, n), 1)

    def over(v, r):
        return jnp.broadcast_to(v[r % 8 : r % 8 + 1, :], (8, n))

    for first in range(start, stop, h):
        tiles = [a[first + 8 * i : first + 8 * i + 8, :] for i in range(h // 8)]
        d = None
        for k in range(first, first + h, b):
            at, off = (k - first) // 8, k % 8
            last = k + b >= first + h
            columns = [
                [jnp.broadcast_to(tile[:, k + s : k + s + 1], (8, n)) for tile in tiles]
                for s in range(b)
            ]
            if d is None:
                d = {(s, t): over(columns[s][at], k + t) for s in range(b) for t in range(s, b)}
            w = dict(d)
            if not last:
                then = (k + b - first) // 8
                for s in range(b):
                    for t in range(b):
                        w[s, b + t] = over(columns[s][then], k + b + t)
                    ahead = jnp.broadcast_to(
                        tiles[then][:, k + b + s : k + b + s + 1], (8, n)
                    )
                    for t in range(s, b):
                        w[b + s, b + t] = over(ahead, k + b + t)
            inside = (lane >= k) & (lane < k + b)
            rows = [
                jnp.where(lane == k + s, 1.0, jnp.where(inside, 0.0, over(tiles[at], off + s)))
                for s in range(b)
            ]
            size = b if last else 2 * b
            w1, turned, (i00, i01, i11), r1 = eliminate(w, 0, size)
            w2, _, (j00, j01, j11), _ = eliminate(w1, 2, size)
            n0 = i00 * rows[0] + i01 * rows[1]
            n1 = i01 * rows[0] + i11 * rows[1]
            m2 = rows[2] - (w[0, 2] * n0 + w[1, 2] * n1)
            m3 = rows[3] - (w[0, 3] * n0 + w[1, 3] * n1)
            n2 = j00 * m2 + j01 * m3
            n3 = j01 * m2 + j11 * m3
            n0 = n0 - (turned[2][0] * r1 * n2 + turned[3][0] * r1 * n3)
            n1 = n1 - (turned[2][1] * r1 * n2 + turned[3][1] * r1 * n3)
            new = [n0, n1, n2, n3]
            if not last:
                d = {(s, t): w2[b + s, b + t] for s in range(b) for t in range(s, b)}
            after = []
            for i, tile in enumerate(tiles):
                c = [columns[s][i] for s in range(b)]
                left = jnp.where(inside, 0.0, tile) - (
                    (c[0] * n0 + c[1] * n1) + (c[2] * n2 + c[3] * n3)
                )
                if i == at:
                    for s in range(b):
                        left = jnp.where(sub == off + s, new[s], left)
                after.append(left)
            tiles = after
        r = jnp.concatenate(tiles, 0)
        inside_n = (lane_n >= first) & (lane_n < first + h)
        rest = jnp.where(inside_n, 0.0, a) - jnp.dot(
            a[:, first : first + h], r, precision=highest, preferred_element_type=f32
        )
        pieces = ([rest[:first]] if first else []) + [r]
        a = jnp.concatenate(pieces + ([rest[first + h :]] if first + h < n else []), 0)
    return a


def block_step(k, p, a, d, left, r):
    n = 128
    row = lax.broadcasted_iota(jnp.int32, (n, n), 0)
    column = lax.broadcasted_iota(jnp.int32, (n, n), 1)
    eye = jnp.where(row == column, 1.0, 0.0)
    at = pl.ds(pl.multiple_of(k * n, n), n)
    then = pl.ds(pl.multiple_of(jnp.minimum(k + 1, kept // n - 1) * n, n), n)
    a[at, at] = -eye
    left[...] = a[:, at]
    a[:, at] = jnp.zeros((kept, n), f32)
    a[at, at] = eye
    r[...] = jnp.dot(p, a[at, :], precision=highest, preferred_element_type=f32)
    a[at, :] = jnp.zeros((n, kept), f32)
    d[...] = a[then, then] - jnp.dot(
        left[then, :], r[:, then], precision=highest, preferred_element_type=f32
    )


def update(a, left, r):
    a[...] -= jnp.dot(left[...], r[...], precision=highest, preferred_element_type=f32)


def mix(keys, q):
    s = lax.dot_general(
        keys[...], q[...], (((1,), (1,)), ((), ())), preferred_element_type=f32
    )
    e = jnp.exp((s - jnp.max(s, axis=0, keepdims=True)) * scale)
    return e / jnp.sum(e, axis=0, keepdims=True)


def gram_kernel(
    flag_ref, index_ref, packets_ref, dense_ref, slot, keys, q_ref, a, d, left, r, dense, mixing
):
    head = spread_index()[0]
    index = index_ref[pl.ds(head, 1), :]
    holder = jnp.broadcast_to(index >> 11, (width, kept))
    down = holder.T
    row = lax.broadcasted_iota(jnp.int32, (kept, width), 0)
    lane = lax.broadcasted_iota(jnp.int32, (kept, width), 1)
    same = jnp.zeros((kept, width), f32)
    for g in range(kept // width):
        across = holder[:1, g * width : (g + 1) * width]
        same += jnp.where((down == across) & (lane + g * width < row), 1.0, 0.0)
    rank = jnp.sum(same, axis=1, keepdims=True)
    own = (down & 15) * 4 + ((down >> 4) ^ head)
    slot[...] = (own * slots).astype(f32) + rank
    sent = packets_ref[:, heads_here:].astype(f32).reshape(count_rows * slots, width).astype(bf16)
    keys[...] = jnp.dot(
        one_hot((down * slots).astype(f32) + rank, count_rows * slots),
        sent,
        preferred_element_type=f32,
    ).astype(bf16)

    @pl.when(flag_ref[0] > 0)
    def _():
        pltpu.sync_copy(dense_ref, dense)
        keys[...] = dense[:, :width]
        slot[...] = dense[:, width:].astype(f32)

    q_ref[...] = packets_ref[:, head].astype(f32).reshape(kept, width).astype(bf16)
    mixing[...] = mix(keys, q_ref)
    row = lax.broadcasted_iota(jnp.int32, (kept, kept), 0)
    column = lax.broadcasted_iota(jnp.int32, (kept, kept), 1)
    a[...] = lax.dot_general(
        mixing[...],
        mixing[...],
        (((1,), (1,)), ((), ())),
        precision=highest,
        preferred_element_type=f32,
    ) + jnp.where(row == column, ridge_weight, 0.0)
    n = 128
    block_step(jnp.int32(0), invert_block(a[:n, :n], n, panel, 0, n), a, d, left, r)
    update(a, left, r)
    d[...] = invert_block(d[...], n, panel, 0, n // 2)


def gram(flag, kept_index, packets, dense):
    n = 128
    return call(
        gram_kernel,
        "gram",
        (
            shape((kept, width), f32),
            shape((kept, width), bf16),
            shape((count_rows * group, width), bf16),
            shape((kept, kept), f32),
            shape((n, n), f32),
        ),
        in_specs=[whole_smem] + [whole_vmem] * 2 + [whole_any],
        out_specs=[whole_vmem] * 5,
        scratch_shapes=[
            pltpu.VMEM((kept, n), f32),
            pltpu.VMEM((n, kept), f32),
            pltpu.VMEM((kept, 2 * width), bf16),
            pltpu.VMEM((kept, kept), f32),
        ],
        cost_estimate=pl.CostEstimate(
            flops=10**10, bytes_accessed=6 * 2**20, transcendentals=2**18
        ),
        compiler_params=params(24),
    )(flag, kept_index, packets, dense)


def in_pieces(x):
    high = x.astype(bf16)
    rest = x - high.astype(f32)
    middle = rest.astype(bf16)
    low = (rest - middle.astype(f32)).astype(bf16)
    return jnp.concatenate([high, middle, low], 0)


def weigh_kernel(
    flag_ref, slot, keys, q, a_ref, d_ref,
    weight_ref, share_ref, plain_ref, a, d, left, r, mixing,
):
    mixing[...] = mix(keys, q)
    a[...] = a_ref[...]
    n = 128
    block_step(jnp.int32(1), invert_block(d_ref[...], n, panel, n // 2, n), a, d, left, r)

    def step(k, _):
        update(a, left, r)
        block_step(k, invert_block(d[...], n, panel, 0, n), a, d, left, r)
        return 0

    lax.fori_loop(2, kept // n, step, 0)
    plane, own = spread_index()
    rows = [pl.ds(pl.multiple_of(128 * (plane ^ k) + 8 * own, 8), 8) for k in range(4)]
    picked = jnp.concatenate([a[at, :] for at in rows], 0)
    picked -= jnp.dot(
        jnp.concatenate([left[at, :] for at in rows], 0),
        r[...],
        precision=highest,
        preferred_element_type=f32,
    )
    weight_ref[...] = in_pieces(
        jnp.dot(picked, mixing[...], precision=highest, preferred_element_type=f32)
    )

    @pl.when(flag_ref[0] == 0)
    def _():
        hot = one_hot(slot[...], count_rows * slots)
        share_ref[...] = jnp.dot(
            in_pieces(ridge_weight * picked), hot, preferred_element_type=f32
        ).astype(bf16)
        plain_ref[...] = jnp.zeros(plain_ref.shape, f32)

    @pl.when(flag_ref[0] > 0)
    def _():
        share_ref[...] = jnp.zeros(share_ref.shape, bf16)
        plain_ref[...] = jnp.dot(
            ridge_weight * picked, slot[...], precision=highest, preferred_element_type=f32
        )


def weigh(flag, *state):
    n = 128
    return call(
        weigh_kernel,
        "weigh",
        (
            shape((96, kept), bf16),
            shape((96, count_rows * slots), bf16),
            shape((32, width), f32),
        ),
        in_specs=[whole_smem] + [whole_vmem] * 5,
        out_specs=[whole_vmem] * 3,
        scratch_shapes=[
            pltpu.VMEM((kept, kept), f32),
            pltpu.VMEM((n, n), f32),
            pltpu.VMEM((kept, n), f32),
            pltpu.VMEM((n, kept), f32),
            pltpu.VMEM((kept, kept), f32),
        ],
        cost_estimate=pl.CostEstimate(
            flops=2 * 10**10, bytes_accessed=6 * 2**20, transcendentals=0
        ),
        compiler_params=params(20),
    )(flag, *state)


def finish_kernel(weight_ref, share_ref, plain_ref, full_ref, sent_ref, *out_refs):
    sent = sent_ref[...].astype(f32)
    targets = [
        jnp.concatenate(
            [sent[:, 4 * i + x].reshape(16 * group, width) for x in range(4)], 0
        )
        for i in range(2)
    ]
    values = sent[:, 8:].reshape(count_rows * slots, width).astype(bf16)
    fitted = jnp.dot(
        weight_ref[...], jnp.concatenate(targets, 1).astype(bf16), preferred_element_type=f32
    )
    shared = jnp.dot(share_ref[...], values, preferred_element_type=f32)
    total = fitted[:, :width] + fitted[:, width:] + shared
    total = total[:32] + total[32:64] + total[64:] + plain_ref[...]
    plane = spread_index()[0]
    for k, out_ref in enumerate(out_refs):
        out_ref[:8] = total[8 * k : 8 * k + 8]
        out_ref[8:] = full_ref[plane ^ k]


def finish(weight, share, plain, full, sent):
    return call(
        finish_kernel,
        "finish",
        [shape((16, width), f32)] * 4,
        in_specs=[whole_vmem] * 5,
        out_specs=[whole_vmem] * 4,
        cost_estimate=pl.CostEstimate(
            flops=2 * 96 * 2560 * 256, bytes_accessed=2**20, transcendentals=0
        ),
        compiler_params=params(10),
    )(weight, share, plain, full, sent)


def arrange_kernel(b0_ref, b1_ref, b2_ref, b3_ref, out_ref, fitted_ref):
    plane = spread_index()[0]
    for k, ref in enumerate((b0_ref, b1_ref, b2_ref, b3_ref)):
        fitted_ref[plane ^ k] = ref[:8]
        out_ref[plane ^ k] = ref[8:].astype(bf16)


def arrange(blocks):
    return call(
        arrange_kernel,
        "arrange",
        (shape((heads_here, group, width), bf16), shape((heads_here, 8, width), f32)),
        in_specs=[whole_vmem] * 4,
        out_specs=[whole_vmem] * 2,
        cost_estimate=pl.CostEstimate(flops=2**13, bytes_accessed=2**16, transcendentals=0),
        compiler_params=params(4),
    )(*blocks)


def dense_rows(kept_index, cache_keys, cache_values):
    local_index = kept_index - own_base()
    inside = (local_index >= 0) & (local_index < local_len)
    at = jnp.clip(local_index, 0, local_len - 1)
    head = jnp.arange(heads_here, dtype=jnp.int32)[:, None]
    rows = jnp.concatenate([cache_keys[at, head], cache_values[at, head]], -1)
    rows = jnp.where(inside[..., None], rows, 0).reshape(count_rows, 32, 2 * width)
    parts = lax.all_to_all(rows, seq_axes, 0, 0)
    found = jnp.sum(parts.astype(f32), axis=0).astype(bf16)
    found = jnp.broadcast_to(found[None], (16,) + found.shape)
    return lax.all_to_all(found, ("y", "z"), 0, 0).reshape(kept, 2 * width)


def along_x(blocks):
    return [blocks[0]] + [
        lax.ppermute(blocks[k], "x", [(i, i ^ k) for i in range(4)]) for k in range(1, 4)
    ]


def on_device(ref_queries, query_pos, cache_keys, cache_values, kept_index):
    keys = cache_keys.reshape(local_len * heads_here, width)
    values = cache_values.reshape(local_len * heads_here, width)
    packets, *kept_values = pack(
        query_pos, kept_index, ref_queries.reshape(heads_here, group, width), keys, values
    )
    packets = lax.all_to_all(packets, seq_axes, 0, 0)
    kept_values = along_x(kept_values)
    parts, flag = attend(packets, keys, values)
    parts = lax.all_to_all(parts, seq_axes, 0, 0)
    dense = lax.cond(
        flag[0] > 0,
        dense_rows,
        lambda *_: jnp.zeros((kept, 2 * width), bf16),
        kept_index,
        cache_keys,
        cache_values,
    )
    state = gram(flag, kept_index, packets, dense)
    full, sent = combine(parts, kept_values)
    sent = lax.all_to_all(sent, ("y", "z"), 0, 0)
    out, fitted = arrange(along_x(finish(*weigh(flag, *state), full, sent)))
    return (out.reshape(1, heads_here * group, width), fitted)


def solution(mesh):
    split = Mesh(mesh.devices.reshape(4, 4, 4, 2), seq_axes + ("head",))
    in_specs = (
        P(seq_axes, "head", None),
        P(seq_axes),
        P(seq_axes, "head", None),
        P(seq_axes, "head", None),
        P("head", None),
    )
    out_specs = (P(seq_axes, "head", None), P("head", seq_axes, None))
    return jax.shard_map(
        on_device, mesh=split, in_specs=in_specs, out_specs=out_specs, check_vma=False
    )
```

```python
import functools
import math

import jax
import jax.numpy as jnp
from jax import lax
from jax.experimental import pallas as pl
from jax.experimental.pallas import tpu as pltpu
from jax.sharding import Mesh, PartitionSpec as P

ridge_weight = 0.01
masked_score = -1e30
highest = lax.Precision.HIGHEST
f32 = jnp.float32
bf16 = jnp.bfloat16

seq_axes = ("x", "y", "z")
count_rows = 64
heads_here = 4
group = 8
width = 128
local_len = 2048
kept = 512
chunk = 1024
slots = 24
slot_tiles = slots // 8
panel = 64
scale = width ** (-0.5)
scale_log2 = scale * math.log2(math.e)


def params(mib):
    return pltpu.CompilerParams(vmem_limit_bytes=mib * 2**20)


def call(kernel, name, out_shape, **more):
    return pl.pallas_call(kernel, name=name, out_shape=out_shape, **more)


def shape(dims, dtype):
    return jax.ShapeDtypeStruct(dims, dtype)


whole_vmem = pl.BlockSpec(memory_space=pltpu.VMEM)
whole_smem = pl.BlockSpec(memory_space=pltpu.SMEM)
whole_any = pl.BlockSpec(memory_space=pl.ANY)
whole_hbm = pl.BlockSpec(memory_space=pltpu.HBM)


def spread_index():
    at = [lax.axis_index(name) for name in seq_axes]
    return at[0], at[1] * 4 + at[2]


def own_base():
    plane, own = spread_index()
    return (plane * 16 + own) * local_len


def pack_kernel(
    pos_ref, index_ref, queries_ref, keys_ref, values_ref, packet_ref, *refs
):
    later_refs, (slot, found, crowd) = refs[:4], refs[4:]
    step = pl.program_id(0)
    rows = chunk * heads_here

    @pl.when(step == 0)
    def _():
        local = index_ref[...] - own_base()
        inside = (local >= 0) & (local < local_len)
        row_id = lax.broadcasted_iota(jnp.int32, (kept, kept), 0)
        lane_id = lax.broadcasted_iota(jnp.int32, (kept, kept), 1)
        before = jnp.where(row_id < lane_id, 1.0, 0.0).astype(bf16)
        rank = jnp.dot(
            jnp.where(inside, 1.0, 0.0).astype(bf16), before, preferred_element_type=f32
        )
        rank = jnp.where(inside, rank, -1.0)
        most = jnp.max(jnp.max(rank, axis=1, keepdims=True), axis=0, keepdims=True)
        crowd[...] = jnp.broadcast_to(jnp.where(most >= slots - 1.0, 1.0, 0.0), crowd.shape)
        spot = (local * heads_here + 1).astype(f32)
        slot_id = lax.broadcasted_iota(jnp.int32, (slots, kept), 0).astype(f32)
        for h in range(heads_here):
            mine = jnp.where(rank[h : h + 1] == slot_id, spot[h : h + 1] + float(h), 0.0)
            taken = jnp.sum(mine, axis=1, keepdims=True) - 1.0
            slot[h * slots : (h + 1) * slots] = jnp.broadcast_to(taken, (slots, width))
        found[...] = jnp.zeros(found.shape, f32)

    found[...] += jnp.dot(
        one_hot(slot[...] - (step * rows).astype(f32), rows),
        jnp.concatenate([keys_ref[...], values_ref[...]], 1),
        preferred_element_type=f32,
    )

    @pl.when(step == local_len // chunk - 1)
    def _():
        at = pos_ref[0]
        sub = lax.broadcasted_iota(jnp.int32, (group, width), 0)
        lane = lax.broadcasted_iota(jnp.int32, (group, width), 1)
        pieces = jnp.where(
            lane == 0, at & 255, jnp.where(lane == 1, (at >> 8) & 255, at >> 16)
        ).astype(f32)
        pieces = jnp.where(lane == 3, crowd[...], pieces)
        for h in range(heads_here):
            sent = found[h * slots : (h + 1) * slots, :width].reshape(slot_tiles, 8, width)
            last = jnp.where(sub == 7, pieces, sent[slot_tiles - 1])
            full = jnp.concatenate(
                [queries_ref[...].astype(f32), sent[: slot_tiles - 1], last[None]], 0
            ).astype(bf16)
            packet_ref[16 * h : 16 * h + 16] = jnp.broadcast_to(full[None], (16,) + full.shape)
        plane = spread_index()[0]
        for k, later_ref in enumerate(later_refs):
            own = pl.ds(pl.multiple_of((plane ^ k) * slots, 8), slots)
            later_ref[...] = found[own, width:].reshape(slot_tiles, 8, width).astype(bf16)


def one_hot(wanted, size):
    lane = lax.broadcasted_iota(jnp.int32, wanted.shape, 1).astype(wanted.dtype)
    return jnp.concatenate(
        [
            jnp.where(wanted == lane + g * width, 1.0, 0.0).astype(bf16)
            for g in range(size // width)
        ],
        1,
    )


def pack(query_pos, kept_index, queries, keys, values):
    rows = chunk * heads_here
    return call(
        pack_kernel,
        "pack",
        (
            shape((count_rows, heads_here + slot_tiles, 8, width), bf16),
        )
        + (shape((slot_tiles, 8, width), bf16),) * 4,
        grid=(local_len // chunk,),
        in_specs=[
            whole_smem,
            pl.BlockSpec((heads_here, kept), lambda i: (0, 0)),
            pl.BlockSpec((heads_here, group, width), lambda i: (0, 0, 0)),
            pl.BlockSpec((rows, width), lambda i: (i, 0)),
            pl.BlockSpec((rows, width), lambda i: (i, 0)),
        ],
        out_specs=[
            pl.BlockSpec(
                (count_rows, heads_here + slot_tiles, 8, width), lambda i: (0, 0, 0, 0)
            ),
        ]
        + [pl.BlockSpec((slot_tiles, 8, width), lambda i: (0, 0, 0))] * 4,
        scratch_shapes=[
            pltpu.VMEM((heads_here * slots, width), f32),
            pltpu.VMEM((heads_here * slots, 2 * width), f32),
            pltpu.VMEM((group, width), f32),
        ],
        cost_estimate=pl.CostEstimate(
            flops=2 * 128 * 8192 * 256, bytes_accessed=5 * 2**20, transcendentals=0
        ),
        compiler_params=params(60),
    )(query_pos, kept_index, queries, keys, values)


def attend_kernel(
    queries_ref, keys_ref, values_ref, packet_ref, flag_ref, raw, wide, keys, values, side, sem
):
    move = pltpu.make_async_copy(values_ref, raw, sem)
    move.start()
    tile = 256
    parts = count_rows * group // tile
    wide[0] = keys_ref[...].astype(f32)
    lane = lax.broadcasted_iota(jnp.int32, (local_len, width), 1)
    lane_t = lax.broadcasted_iota(jnp.int32, (tile, width), 1)
    row_t = lax.broadcasted_iota(jnp.int32, (tile, width), 0)
    pieces = queries_ref[:, heads_here + slot_tiles - 1].astype(f32)[:, 7]
    flag_ref[0] = (jnp.max(pieces[:, 3:4]) > 0.0).astype(jnp.int32)
    row_id = lax.broadcasted_iota(jnp.int32, (count_rows, width), 0)
    lane_id = lax.broadcasted_iota(jnp.int32, (count_rows, width), 1)
    place = pieces[:, 0:1] + 256.0 * pieces[:, 1:2] + 65536.0 * pieces[:, 2:3]
    place = jnp.sum(jnp.where(row_id == lane_id, place, 0.0), axis=0, keepdims=True)
    spot = lax.broadcasted_iota(jnp.int32, (local_len, width), 0) + own_base()
    late = (spot.astype(f32) > place) & (lane < count_rows)
    late = jnp.where(late, masked_score, 0.0).astype(bf16)
    ones = jnp.where(lane == 0, 1.0, 0.0).astype(bf16)
    for i in range(2):
        keys[i, :, width:] = late
        values[i, :, width:] = ones
    side[...] = jnp.zeros(side.shape, f32)

    def scores(h, part):
        if part == 0:
            at = pl.ds(h, local_len, stride=heads_here)
            keys[h % 2, :, :width] = wide[0, at, :].astype(bf16)
        rows = tile // group
        q = queries_ref[part * rows : (part + 1) * rows, h].astype(f32).reshape(tile, width)
        own = jnp.where(row_t // group + part * rows == lane_t, 1.0, 0.0)
        q = jnp.concatenate([q, own], 1).astype(bf16)
        return lax.dot_general(
            q, keys[h % 2], (((1,), (1,)), ((), ())), preferred_element_type=f32
        )

    steps = [(h, part) for h in range(heads_here) for part in range(parts)]
    s = scores(*steps[0])
    for i, (h, part) in enumerate(steps):
        after = scores(*steps[i + 1]) if i + 1 < len(steps) else None
        peak = jnp.max(s, axis=1, keepdims=True)
        w = jnp.exp2((s - peak) * scale_log2).astype(bf16)
        if i == 0:
            move.wait()
            wide[1] = raw[...].astype(f32)
        if part == 0:
            at = pl.ds(h, local_len, stride=heads_here)
            values[h % 2, :, :width] = wide[1, at, :].astype(bf16)
        o = jnp.dot(w, values[h % 2], preferred_element_type=f32)
        sums = o[:, width : width + 1]
        mass = peak * scale_log2 + jnp.log2(sums)
        high = mass.astype(bf16).astype(f32)
        middle = (mass - high).astype(bf16).astype(f32)
        low = mass - high - middle
        first = 3 * (row_t // 128 + part * 2)
        mark = jnp.where(
            lane_t == first,
            high,
            jnp.where(lane_t == first + 1, middle, jnp.where(lane_t == first + 2, low, 0.0)),
        )
        to = slice(16 * h, 16 * h + 16)
        mark = mark.reshape(2, 16, group, width)
        done = (o[:, :width] / sums).reshape(2, 16, group, width).astype(bf16)
        for x in range(2):
            packet_ref[to, 2 * part + x] = done[x]
        side[to] += mark[0] + mark[1]
        s = after
    packet_ref[:, 4] = side[...].astype(bf16)


def attend(packets, keys, values):
    return call(
        attend_kernel,
        "attend",
        (
            shape((count_rows, heads_here + 1, group, width), bf16),
            shape((1,), jnp.int32),
        ),
        in_specs=[whole_vmem] * 2 + [whole_hbm],
        out_specs=[whole_vmem, whole_smem],
        scratch_shapes=[
            pltpu.VMEM((local_len * heads_here, width), bf16),
            pltpu.VMEM((2, local_len * heads_here, width), f32),
            pltpu.VMEM((2, local_len, 2 * width), bf16),
            pltpu.VMEM((2, local_len, 2 * width), bf16),
            pltpu.VMEM((count_rows, group, width), f32),
            pltpu.SemaphoreType.DMA,
        ],
        cost_estimate=pl.CostEstimate(
            flops=2 * 2 * 512 * 2048 * 256 * 4,
            bytes_accessed=6 * 2**20,
            transcendentals=4 * 512 * 2048,
        ),
        compiler_params=params(36),
    )(packets, keys, values)


def combine_kernel(parts_ref, v0_ref, v1_ref, v2_ref, v3_ref, full_ref, spread_ref):
    side = parts_ref[:, 4].astype(f32)
    lane = lax.broadcasted_iota(jnp.int32, side.shape, 2)
    for i in range(4):
        part = parts_ref[:, i].astype(f32)
        own = (lane >= 3 * i) & (lane < 3 * i + 3)
        mass = jnp.sum(jnp.where(own, side, 0.0), axis=2, keepdims=True)
        top = jnp.max(mass, axis=0, keepdims=True)
        share = jnp.exp2(mass - top)
        full = jnp.sum(share * part, axis=0) / jnp.sum(share, axis=0)
        full_ref[i] = full
        high = full.astype(bf16)
        low = (full - high.astype(f32)).astype(bf16)
        spread_ref[:, i] = jnp.broadcast_to(high[None], (16, group, width))
        spread_ref[:, 4 + i] = jnp.broadcast_to(low[None], (16, group, width))
    for k, ref in enumerate((v0_ref, v1_ref, v2_ref, v3_ref)):
        at = 8 + k * slot_tiles
        spread_ref[:, at : at + slot_tiles] = jnp.broadcast_to(
            ref[...][None], (16, slot_tiles, 8, width)
        )


def combine(parts, kept_values):
    return call(
        combine_kernel,
        "combine",
        (
            shape((4, group, width), f32),
            shape((16, 8 + 4 * slot_tiles, group, width), bf16),
        ),
        in_specs=[whole_vmem] * 5,
        out_specs=[whole_vmem] * 2,
        cost_estimate=pl.CostEstimate(
            flops=2 * 2**20, bytes_accessed=2 * 2**20, transcendentals=2048
        ),
        compiler_params=params(12),
    )(parts, *kept_values)


def reciprocal(x):
    r = pltpu.reciprocal(x, approx=True)
    return r * (2.0 - x * r)


def eliminate(w, o, size):
    p, q, s = w[o, o], w[o, o + 1], w[o + 1, o + 1]
    r = reciprocal(p * s - q * q)
    side = range(o + 2, size)
    turned = {u: (s * w[o, u] - q * w[o + 1, u], p * w[o + 1, u] - q * w[o, u]) for u in side}
    left = {}
    for u in side:
        for v in range(u, size):
            left[u, v] = w[u, v] - (w[o, u] * turned[v][0] + w[o + 1, u] * turned[v][1]) * r
    return left, turned, (s * r, -q * r, p * r), r


def invert_block(a, n, h, start, stop):
    b = 4
    lane = lax.broadcasted_iota(jnp.int32, (8, n), 1)
    sub = lax.broadcasted_iota(jnp.int32, (8, n), 0)
    lane_n = lax.broadcasted_iota(jnp.int32, (n, n), 1)

    def over(v, r):
        return jnp.broadcast_to(v[r % 8 : r % 8 + 1, :], (8, n))

    for first in range(start, stop, h):
        tiles = [a[first + 8 * i : first + 8 * i + 8, :] for i in range(h // 8)]
        d = None
        for k in range(first, first + h, b):
            at, off = (k - first) // 8, k % 8
            last = k + b >= first + h
            columns = [
                [jnp.broadcast_to(tile[:, k + s : k + s + 1], (8, n)) for tile in tiles]
                for s in range(b)
            ]
            if d is None:
                d = {(s, t): over(columns[s][at], k + t) for s in range(b) for t in range(s, b)}
            w = dict(d)
            if not last:
                then = (k + b - first) // 8
                for s in range(b):
                    for t in range(b):
                        w[s, b + t] = over(columns[s][then], k + b + t)
                    ahead = jnp.broadcast_to(
                        tiles[then][:, k + b + s : k + b + s + 1], (8, n)
                    )
                    for t in range(s, b):
                        w[b + s, b + t] = over(ahead, k + b + t)
            inside = (lane >= k) & (lane < k + b)
            rows = [
                jnp.where(lane == k + s, 1.0, jnp.where(inside, 0.0, over(tiles[at], off + s)))
                for s in range(b)
            ]
            size = b if last else 2 * b
            w1, turned, (i00, i01, i11), r1 = eliminate(w, 0, size)
            w2, _, (j00, j01, j11), _ = eliminate(w1, 2, size)
            n0 = i00 * rows[0] + i01 * rows[1]
            n1 = i01 * rows[0] + i11 * rows[1]
            m2 = rows[2] - (w[0, 2] * n0 + w[1, 2] * n1)
            m3 = rows[3] - (w[0, 3] * n0 + w[1, 3] * n1)
            n2 = j00 * m2 + j01 * m3
            n3 = j01 * m2 + j11 * m3
            n0 = n0 - (turned[2][0] * r1 * n2 + turned[3][0] * r1 * n3)
            n1 = n1 - (turned[2][1] * r1 * n2 + turned[3][1] * r1 * n3)
            new = [n0, n1, n2, n3]
            if not last:
                d = {(s, t): w2[b + s, b + t] for s in range(b) for t in range(s, b)}
            after = []
            for i, tile in enumerate(tiles):
                c = [columns[s][i] for s in range(b)]
                left = jnp.where(inside, 0.0, tile) - (
                    (c[0] * n0 + c[1] * n1) + (c[2] * n2 + c[3] * n3)
                )
                if i == at:
                    for s in range(b):
                        left = jnp.where(sub == off + s, new[s], left)
                after.append(left)
            tiles = after
        r = jnp.concatenate(tiles, 0)
        inside_n = (lane_n >= first) & (lane_n < first + h)
        rest = jnp.where(inside_n, 0.0, a) - jnp.dot(
            a[:, first : first + h], r, precision=highest, preferred_element_type=f32
        )
        pieces = ([rest[:first]] if first else []) + [r]
        a = jnp.concatenate(pieces + ([rest[first + h :]] if first + h < n else []), 0)
    return a


def block_step(k, p, a, d, left, r):
    n = 128
    row = lax.broadcasted_iota(jnp.int32, (n, n), 0)
    column = lax.broadcasted_iota(jnp.int32, (n, n), 1)
    eye = jnp.where(row == column, 1.0, 0.0)
    at = pl.ds(pl.multiple_of(k * n, n), n)
    then = pl.ds(pl.multiple_of(jnp.minimum(k + 1, kept // n - 1) * n, n), n)
    a[at, at] = -eye
    left[...] = a[:, at]
    a[:, at] = jnp.zeros((kept, n), f32)
    a[at, at] = eye
    r[...] = jnp.dot(p, a[at, :], precision=highest, preferred_element_type=f32)
    a[at, :] = jnp.zeros((n, kept), f32)
    d[...] = a[then, then] - jnp.dot(
        left[then, :], r[:, then], precision=highest, preferred_element_type=f32
    )


def update(a, left, r):
    a[...] -= jnp.dot(left[...], r[...], precision=highest, preferred_element_type=f32)


def mix(keys, q):
    s = lax.dot_general(
        keys[...], q[...], (((1,), (1,)), ((), ())), preferred_element_type=f32
    )
    e = jnp.exp((s - jnp.max(s, axis=0, keepdims=True)) * scale)
    return e / jnp.sum(e, axis=0, keepdims=True)


def gram_kernel(
    flag_ref, index_ref, packets_ref, dense_ref, slot, keys, q_ref, a, d, left, r, dense, mixing
):
    head = spread_index()[0]
    index = index_ref[pl.ds(head, 1), :]
    holder = jnp.broadcast_to(index >> 11, (width, kept))
    down = holder.T
    row = lax.broadcasted_iota(jnp.int32, (kept, width), 0)
    lane = lax.broadcasted_iota(jnp.int32, (kept, width), 1)
    same = jnp.zeros((kept, width), f32)
    for g in range(kept // width):
        across = holder[:1, g * width : (g + 1) * width]
        same += jnp.where((down == across) & (lane + g * width < row), 1.0, 0.0)
    rank = jnp.sum(same, axis=1, keepdims=True)
    own = (down & 15) * 4 + ((down >> 4) ^ head)
    slot[...] = (own * slots).astype(f32) + rank
    sent = packets_ref[:, heads_here:].astype(f32).reshape(count_rows * slots, width).astype(bf16)
    keys[...] = jnp.dot(
        one_hot((down * slots).astype(f32) + rank, count_rows * slots),
        sent,
        preferred_element_type=f32,
    ).astype(bf16)

    @pl.when(flag_ref[0] > 0)
    def _():
        pltpu.sync_copy(dense_ref, dense)
        keys[...] = dense[:, :width]
        slot[...] = dense[:, width:].astype(f32)

    q_ref[...] = packets_ref[:, head].astype(f32).reshape(kept, width).astype(bf16)
    mixing[...] = mix(keys, q_ref)
    row = lax.broadcasted_iota(jnp.int32, (kept, kept), 0)
    column = lax.broadcasted_iota(jnp.int32, (kept, kept), 1)
    a[...] = lax.dot_general(
        mixing[...],
        mixing[...],
        (((1,), (1,)), ((), ())),
        precision=highest,
        preferred_element_type=f32,
    ) + jnp.where(row == column, ridge_weight, 0.0)
    n = 128
    block_step(jnp.int32(0), invert_block(a[:n, :n], n, panel, 0, n), a, d, left, r)
    update(a, left, r)
    d[...] = invert_block(d[...], n, 32, 0, 96)


def gram(flag, kept_index, packets, dense):
    n = 128
    return call(
        gram_kernel,
        "gram",
        (
            shape((kept, width), f32),
            shape((kept, width), bf16),
            shape((count_rows * group, width), bf16),
            shape((kept, kept), f32),
            shape((n, n), f32),
        ),
        in_specs=[whole_smem] + [whole_vmem] * 2 + [whole_any],
        out_specs=[whole_vmem] * 5,
        scratch_shapes=[
            pltpu.VMEM((kept, n), f32),
            pltpu.VMEM((n, kept), f32),
            pltpu.VMEM((kept, 2 * width), bf16),
            pltpu.VMEM((kept, kept), f32),
        ],
        cost_estimate=pl.CostEstimate(
            flops=10**10, bytes_accessed=6 * 2**20, transcendentals=2**18
        ),
        compiler_params=params(24),
    )(flag, kept_index, packets, dense)


def in_pieces(x):
    high = x.astype(bf16)
    rest = x - high.astype(f32)
    middle = rest.astype(bf16)
    low = (rest - middle.astype(f32)).astype(bf16)
    return jnp.concatenate([high, middle, low], 0)


def weigh_kernel(
    flag_ref, slot, keys, q, a_ref, d_ref,
    weight_ref, share_ref, plain_ref, a, d, left, r, mixing,
):
    mixing[...] = mix(keys, q)
    a[...] = a_ref[...]
    n = 128
    block_step(jnp.int32(1), invert_block(d_ref[...], n, 32, 96, n), a, d, left, r)

    def step(k, _):
        update(a, left, r)
        block_step(k, invert_block(d[...], n, panel, 0, n), a, d, left, r)
        return 0

    lax.fori_loop(2, kept // n, step, 0)
    plane, own = spread_index()
    rows = [pl.ds(pl.multiple_of(128 * (plane ^ k) + 8 * own, 8), 8) for k in range(4)]
    picked = jnp.concatenate([a[at, :] for at in rows], 0)
    picked -= jnp.dot(
        jnp.concatenate([left[at, :] for at in rows], 0),
        r[...],
        precision=highest,
        preferred_element_type=f32,
    )
    weight_ref[...] = in_pieces(
        jnp.dot(picked, mixing[...], precision=highest, preferred_element_type=f32)
    )

    @pl.when(flag_ref[0] == 0)
    def _():
        hot = one_hot(slot[...], count_rows * slots)
        share_ref[...] = jnp.dot(
            in_pieces(ridge_weight * picked), hot, preferred_element_type=f32
        ).astype(bf16)
        plain_ref[...] = jnp.zeros(plain_ref.shape, f32)

    @pl.when(flag_ref[0] > 0)
    def _():
        share_ref[...] = jnp.zeros(share_ref.shape, bf16)
        plain_ref[...] = jnp.dot(
            ridge_weight * picked, slot[...], precision=highest, preferred_element_type=f32
        )


def weigh(flag, *state):
    n = 128
    return call(
        weigh_kernel,
        "weigh",
        (
            shape((96, kept), bf16),
            shape((96, count_rows * slots), bf16),
            shape((32, width), f32),
        ),
        in_specs=[whole_smem] + [whole_vmem] * 5,
        out_specs=[whole_vmem] * 3,
        scratch_shapes=[
            pltpu.VMEM((kept, kept), f32),
            pltpu.VMEM((n, n), f32),
            pltpu.VMEM((kept, n), f32),
            pltpu.VMEM((n, kept), f32),
            pltpu.VMEM((kept, kept), f32),
        ],
        cost_estimate=pl.CostEstimate(
            flops=2 * 10**10, bytes_accessed=6 * 2**20, transcendentals=0
        ),
        compiler_params=params(20),
    )(flag, *state)


def finish_kernel(weight_ref, share_ref, plain_ref, full_ref, sent_ref, *out_refs):
    sent = sent_ref[...].astype(f32)
    targets = [
        jnp.concatenate(
            [sent[:, 4 * i + x].reshape(16 * group, width) for x in range(4)], 0
        )
        for i in range(2)
    ]
    values = sent[:, 8:].reshape(count_rows * slots, width).astype(bf16)
    fitted = jnp.dot(
        weight_ref[...], jnp.concatenate(targets, 1).astype(bf16), preferred_element_type=f32
    )
    shared = jnp.dot(share_ref[...], values, preferred_element_type=f32)
    total = fitted[:, :width] + fitted[:, width:] + shared
    total = total[:32] + total[32:64] + total[64:] + plain_ref[...]
    plane = spread_index()[0]
    for k, out_ref in enumerate(out_refs):
        out_ref[:8] = total[8 * k : 8 * k + 8]
        out_ref[8:] = full_ref[plane ^ k]


def finish(weight, share, plain, full, sent):
    return call(
        finish_kernel,
        "finish",
        [shape((16, width), f32)] * 4,
        in_specs=[whole_vmem] * 5,
        out_specs=[whole_vmem] * 4,
        cost_estimate=pl.CostEstimate(
            flops=2 * 96 * 2560 * 256, bytes_accessed=2**20, transcendentals=0
        ),
        compiler_params=params(10),
    )(weight, share, plain, full, sent)


def arrange_kernel(b0_ref, b1_ref, b2_ref, b3_ref, out_ref, fitted_ref):
    plane = spread_index()[0]
    for k, ref in enumerate((b0_ref, b1_ref, b2_ref, b3_ref)):
        fitted_ref[plane ^ k] = ref[:8]
        out_ref[plane ^ k] = ref[8:].astype(bf16)


def arrange(blocks):
    return call(
        arrange_kernel,
        "arrange",
        (shape((heads_here, group, width), bf16), shape((heads_here, 8, width), f32)),
        in_specs=[whole_vmem] * 4,
        out_specs=[whole_vmem] * 2,
        cost_estimate=pl.CostEstimate(flops=2**13, bytes_accessed=2**16, transcendentals=0),
        compiler_params=params(4),
    )(*blocks)


def dense_rows(kept_index, cache_keys, cache_values):
    local_index = kept_index - own_base()
    inside = (local_index >= 0) & (local_index < local_len)
    at = jnp.clip(local_index, 0, local_len - 1)
    head = jnp.arange(heads_here, dtype=jnp.int32)[:, None]
    rows = jnp.concatenate([cache_keys[at, head], cache_values[at, head]], -1)
    rows = jnp.where(inside[..., None], rows, 0).reshape(count_rows, 32, 2 * width)
    parts = lax.all_to_all(rows, seq_axes, 0, 0)
    found = jnp.sum(parts.astype(f32), axis=0).astype(bf16)
    found = jnp.broadcast_to(found[None], (16,) + found.shape)
    return lax.all_to_all(found, ("y", "z"), 0, 0).reshape(kept, 2 * width)


def along_x(blocks):
    return [blocks[0]] + [
        lax.ppermute(blocks[k], "x", [(i, i ^ k) for i in range(4)]) for k in range(1, 4)
    ]


def on_device(ref_queries, query_pos, cache_keys, cache_values, kept_index):
    keys = cache_keys.reshape(local_len * heads_here, width)
    values = cache_values.reshape(local_len * heads_here, width)
    packets, *kept_values = pack(
        query_pos, kept_index, ref_queries.reshape(heads_here, group, width), keys, values
    )
    packets = lax.all_to_all(packets, seq_axes, 0, 0)
    kept_values = along_x(kept_values)
    parts, flag = attend(packets, keys, values)
    parts = lax.all_to_all(parts, seq_axes, 0, 0)
    dense = lax.cond(
        flag[0] > 0,
        dense_rows,
        lambda *_: jnp.zeros((kept, 2 * width), bf16),
        kept_index,
        cache_keys,
        cache_values,
    )
    state = gram(flag, kept_index, packets, dense)
    full, sent = combine(parts, kept_values)
    sent = lax.all_to_all(sent, ("y", "z"), 0, 0)
    out, fitted = arrange(along_x(finish(*weigh(flag, *state), full, sent)))
    return (out.reshape(1, heads_here * group, width), fitted)


def solution(mesh):
    split = Mesh(mesh.devices.reshape(4, 4, 4, 2), seq_axes + ("head",))
    in_specs = (
        P(seq_axes, "head", None),
        P(seq_axes),
        P(seq_axes, "head", None),
        P(seq_axes, "head", None),
        P("head", None),
    )
    out_specs = (P(seq_axes, "head", None), P("head", seq_axes, None))
    return jax.shard_map(
        on_device, mesh=split, in_specs=in_specs, out_specs=out_specs, check_vma=False
    )
```

```python
import functools
import math

import jax
import jax.numpy as jnp
from jax import lax
from jax.experimental import pallas as pl
from jax.experimental.pallas import tpu as pltpu
from jax.sharding import Mesh, PartitionSpec as P

ridge_weight = 0.01
masked_score = -1e30
highest = lax.Precision.HIGHEST
f32 = jnp.float32
bf16 = jnp.bfloat16

seq_axes = ("x", "y", "z")
count_rows = 64
heads_here = 4
group = 8
width = 128
local_len = 2048
kept = 512
chunk = 1024
slots = 24
slot_tiles = slots // 8
panel = 64
scale = width ** (-0.5)
scale_log2 = scale * math.log2(math.e)


def params(mib):
    return pltpu.CompilerParams(vmem_limit_bytes=mib * 2**20)


def call(kernel, name, out_shape, **more):
    return pl.pallas_call(kernel, name=name, out_shape=out_shape, **more)


def shape(dims, dtype):
    return jax.ShapeDtypeStruct(dims, dtype)


whole_vmem = pl.BlockSpec(memory_space=pltpu.VMEM)
whole_smem = pl.BlockSpec(memory_space=pltpu.SMEM)
whole_any = pl.BlockSpec(memory_space=pl.ANY)
whole_hbm = pl.BlockSpec(memory_space=pltpu.HBM)


def spread_index():
    at = [lax.axis_index(name) for name in seq_axes]
    return at[0], at[1] * 4 + at[2]


def own_base():
    plane, own = spread_index()
    return (plane * 16 + own) * local_len


def pack_kernel(
    pos_ref, index_ref, queries_ref, keys_ref, values_ref, packet_ref, *refs
):
    later_refs, (slot, found, crowd) = refs[:4], refs[4:]
    step = pl.program_id(0)
    rows = chunk * heads_here

    @pl.when(step == 0)
    def _():
        local = index_ref[...] - own_base()
        inside = (local >= 0) & (local < local_len)
        row_id = lax.broadcasted_iota(jnp.int32, (kept, kept), 0)
        lane_id = lax.broadcasted_iota(jnp.int32, (kept, kept), 1)
        before = jnp.where(row_id < lane_id, 1.0, 0.0).astype(bf16)
        rank = jnp.dot(
            jnp.where(inside, 1.0, 0.0).astype(bf16), before, preferred_element_type=f32
        )
        rank = jnp.where(inside, rank, -1.0)
        most = jnp.max(jnp.max(rank, axis=1, keepdims=True), axis=0, keepdims=True)
        crowd[...] = jnp.broadcast_to(jnp.where(most >= slots - 1.0, 1.0, 0.0), crowd.shape)
        spot = (local * heads_here + 1).astype(f32)
        slot_id = lax.broadcasted_iota(jnp.int32, (slots, kept), 0).astype(f32)
        for h in range(heads_here):
            mine = jnp.where(rank[h : h + 1] == slot_id, spot[h : h + 1] + float(h), 0.0)
            taken = jnp.sum(mine, axis=1, keepdims=True) - 1.0
            slot[h * slots : (h + 1) * slots] = jnp.broadcast_to(taken, (slots, width))
        found[...] = jnp.zeros(found.shape, f32)

    found[...] += jnp.dot(
        one_hot(slot[...] - (step * rows).astype(f32), rows),
        jnp.concatenate([keys_ref[...], values_ref[...]], 1),
        preferred_element_type=f32,
    )

    @pl.when(step == local_len // chunk - 1)
    def _():
        at = pos_ref[0]
        sub = lax.broadcasted_iota(jnp.int32, (group, width), 0)
        lane = lax.broadcasted_iota(jnp.int32, (group, width), 1)
        pieces = jnp.where(
            lane == 0, at & 255, jnp.where(lane == 1, (at >> 8) & 255, at >> 16)
        ).astype(f32)
        pieces = jnp.where(lane == 3, crowd[...], pieces)
        for h in range(heads_here):
            sent = found[h * slots : (h + 1) * slots, :width].reshape(slot_tiles, 8, width)
            last = jnp.where(sub == 7, pieces, sent[slot_tiles - 1])
            full = jnp.concatenate(
                [queries_ref[...].astype(f32), sent[: slot_tiles - 1], last[None]], 0
            ).astype(bf16)
            packet_ref[16 * h : 16 * h + 16] = jnp.broadcast_to(full[None], (16,) + full.shape)
        plane = spread_index()[0]
        for k, later_ref in enumerate(later_refs):
            own = pl.ds(pl.multiple_of((plane ^ k) * slots, 8), slots)
            later_ref[...] = found[own, width:].reshape(slot_tiles, 8, width).astype(bf16)


def one_hot(wanted, size):
    lane = lax.broadcasted_iota(jnp.int32, wanted.shape, 1).astype(wanted.dtype)
    return jnp.concatenate(
        [
            jnp.where(wanted == lane + g * width, 1.0, 0.0).astype(bf16)
            for g in range(size // width)
        ],
        1,
    )


def pack(query_pos, kept_index, queries, keys, values):
    rows = chunk * heads_here
    return call(
        pack_kernel,
        "pack",
        (
            shape((count_rows, heads_here + slot_tiles, 8, width), bf16),
        )
        + (shape((slot_tiles, 8, width), bf16),) * 4,
        grid=(local_len // chunk,),
        in_specs=[
            whole_smem,
            pl.BlockSpec((heads_here, kept), lambda i: (0, 0)),
            pl.BlockSpec((heads_here, group, width), lambda i: (0, 0, 0)),
            pl.BlockSpec((rows, width), lambda i: (i, 0)),
            pl.BlockSpec((rows, width), lambda i: (i, 0)),
        ],
        out_specs=[
            pl.BlockSpec(
                (count_rows, heads_here + slot_tiles, 8, width), lambda i: (0, 0, 0, 0)
            ),
        ]
        + [pl.BlockSpec((slot_tiles, 8, width), lambda i: (0, 0, 0))] * 4,
        scratch_shapes=[
            pltpu.VMEM((heads_here * slots, width), f32),
            pltpu.VMEM((heads_here * slots, 2 * width), f32),
            pltpu.VMEM((group, width), f32),
        ],
        cost_estimate=pl.CostEstimate(
            flops=2 * 128 * 8192 * 256, bytes_accessed=5 * 2**20, transcendentals=0
        ),
        compiler_params=params(60),
    )(query_pos, kept_index, queries, keys, values)


def attend_kernel(
    queries_ref, keys_ref, values_ref, packet_ref, flag_ref, raw, wide, keys, values, side, sem
):
    move = pltpu.make_async_copy(values_ref, raw, sem)
    move.start()
    tile = 256
    parts = count_rows * group // tile
    wide[0] = keys_ref[...].astype(f32)
    lane = lax.broadcasted_iota(jnp.int32, (local_len, width), 1)
    lane_t = lax.broadcasted_iota(jnp.int32, (tile, width), 1)
    row_t = lax.broadcasted_iota(jnp.int32, (tile, width), 0)
    pieces = queries_ref[:, heads_here + slot_tiles - 1].astype(f32)[:, 7]
    flag_ref[0] = (jnp.max(pieces[:, 3:4]) > 0.0).astype(jnp.int32)
    row_id = lax.broadcasted_iota(jnp.int32, (count_rows, width), 0)
    lane_id = lax.broadcasted_iota(jnp.int32, (count_rows, width), 1)
    place = pieces[:, 0:1] + 256.0 * pieces[:, 1:2] + 65536.0 * pieces[:, 2:3]
    place = jnp.sum(jnp.where(row_id == lane_id, place, 0.0), axis=0, keepdims=True)
    spot = lax.broadcasted_iota(jnp.int32, (local_len, width), 0) + own_base()
    late = (spot.astype(f32) > place) & (lane < count_rows)
    late = jnp.where(late, masked_score, 0.0).astype(bf16)
    ones = jnp.where(lane == 0, 1.0, 0.0).astype(bf16)
    for i in range(2):
        keys[i, :, width:] = late
        values[i, :, width:] = ones
    side[...] = jnp.zeros(side.shape, f32)

    def scores(h, part):
        if part == 0:
            at = pl.ds(h, local_len, stride=heads_here)
            keys[h % 2, :, :width] = wide[0, at, :].astype(bf16)
        rows = tile // group
        q = queries_ref[part * rows : (part + 1) * rows, h].astype(f32).reshape(tile, width)
        own = jnp.where(row_t // group + part * rows == lane_t, 1.0, 0.0)
        q = jnp.concatenate([q, own], 1).astype(bf16)
        return lax.dot_general(
            q, keys[h % 2], (((1,), (1,)), ((), ())), preferred_element_type=f32
        )

    steps = [(h, part) for h in range(heads_here) for part in range(parts)]
    s = scores(*steps[0])
    for i, (h, part) in enumerate(steps):
        after = scores(*steps[i + 1]) if i + 1 < len(steps) else None
        peak = jnp.max(s, axis=1, keepdims=True)
        w = jnp.exp2((s - peak) * scale_log2).astype(bf16)
        if i == 0:
            move.wait()
            wide[1] = raw[...].astype(f32)
        if part == 0:
            at = pl.ds(h, local_len, stride=heads_here)
            values[h % 2, :, :width] = wide[1, at, :].astype(bf16)
        o = jnp.dot(w, values[h % 2], preferred_element_type=f32)
        sums = o[:, width : width + 1]
        mass = peak * scale_log2 + jnp.log2(sums)
        high = mass.astype(bf16).astype(f32)
        middle = (mass - high).astype(bf16).astype(f32)
        low = mass - high - middle
        first = 3 * (row_t // 128 + part * 2)
        mark = jnp.where(
            lane_t == first,
            high,
            jnp.where(lane_t == first + 1, middle, jnp.where(lane_t == first + 2, low, 0.0)),
        )
        to = slice(16 * h, 16 * h + 16)
        mark = mark.reshape(2, 16, group, width)
        done = (o[:, :width] / sums).reshape(2, 16, group, width).astype(bf16)
        for x in range(2):
            packet_ref[to, 2 * part + x] = done[x]
        side[to] += mark[0] + mark[1]
        s = after
    packet_ref[:, 4] = side[...].astype(bf16)


def attend(packets, keys, values):
    return call(
        attend_kernel,
        "attend",
        (
            shape((count_rows, heads_here + 1, group, width), bf16),
            shape((1,), jnp.int32),
        ),
        in_specs=[whole_vmem] * 2 + [whole_hbm],
        out_specs=[whole_vmem, whole_smem],
        scratch_shapes=[
            pltpu.VMEM((local_len * heads_here, width), bf16),
            pltpu.VMEM((2, local_len * heads_here, width), f32),
            pltpu.VMEM((2, local_len, 2 * width), bf16),
            pltpu.VMEM((2, local_len, 2 * width), bf16),
            pltpu.VMEM((count_rows, group, width), f32),
            pltpu.SemaphoreType.DMA,
        ],
        cost_estimate=pl.CostEstimate(
            flops=2 * 2 * 512 * 2048 * 256 * 4,
            bytes_accessed=6 * 2**20,
            transcendentals=4 * 512 * 2048,
        ),
        compiler_params=params(36),
    )(packets, keys, values)


def combine_kernel(parts_ref, v0_ref, v1_ref, v2_ref, v3_ref, full_ref, spread_ref):
    side = parts_ref[:, 4].astype(f32)
    lane = lax.broadcasted_iota(jnp.int32, side.shape, 2)
    for i in range(4):
        part = parts_ref[:, i].astype(f32)
        own = (lane >= 3 * i) & (lane < 3 * i + 3)
        mass = jnp.sum(jnp.where(own, side, 0.0), axis=2, keepdims=True)
        top = jnp.max(mass, axis=0, keepdims=True)
        share = jnp.exp2(mass - top)
        full = jnp.sum(share * part, axis=0) / jnp.sum(share, axis=0)
        full_ref[i] = full
        high = full.astype(bf16)
        low = (full - high.astype(f32)).astype(bf16)
        spread_ref[:, i] = jnp.broadcast_to(high[None], (16, group, width))
        spread_ref[:, 4 + i] = jnp.broadcast_to(low[None], (16, group, width))
    for k, ref in enumerate((v0_ref, v1_ref, v2_ref, v3_ref)):
        at = 8 + k * slot_tiles
        spread_ref[:, at : at + slot_tiles] = jnp.broadcast_to(
            ref[...][None], (16, slot_tiles, 8, width)
        )


def combine(parts, kept_values):
    return call(
        combine_kernel,
        "combine",
        (
            shape((4, group, width), f32),
            shape((16, 8 + 4 * slot_tiles, group, width), bf16),
        ),
        in_specs=[whole_vmem] * 5,
        out_specs=[whole_vmem] * 2,
        cost_estimate=pl.CostEstimate(
            flops=2 * 2**20, bytes_accessed=2 * 2**20, transcendentals=2048
        ),
        compiler_params=params(12),
    )(parts, *kept_values)


def reciprocal(x):
    r = pltpu.reciprocal(x, approx=True)
    return r * (2.0 - x * r)


def eliminate(w, o, size):
    p, q, s = w[o, o], w[o, o + 1], w[o + 1, o + 1]
    r = reciprocal(p * s - q * q)
    side = range(o + 2, size)
    turned = {u: (s * w[o, u] - q * w[o + 1, u], p * w[o + 1, u] - q * w[o, u]) for u in side}
    left = {}
    for u in side:
        for v in range(u, size):
            left[u, v] = w[u, v] - (w[o, u] * turned[v][0] + w[o + 1, u] * turned[v][1]) * r
    return left, turned, (s * r, -q * r, p * r), r


def invert_block(a, n, h, start, stop):
    b = 4
    lane = lax.broadcasted_iota(jnp.int32, (8, n), 1)
    sub = lax.broadcasted_iota(jnp.int32, (8, n), 0)
    lane_n = lax.broadcasted_iota(jnp.int32, (n, n), 1)

    def over(v, r):
        return jnp.broadcast_to(v[r % 8 : r % 8 + 1, :], (8, n))

    for first in range(start, stop, h):
        tiles = [a[first + 8 * i : first + 8 * i + 8, :] for i in range(h // 8)]
        d = None
        for k in range(first, first + h, b):
            at, off = (k - first) // 8, k % 8
            last = k + b >= first + h
            columns = [
                [jnp.broadcast_to(tile[:, k + s : k + s + 1], (8, n)) for tile in tiles]
                for s in range(b)
            ]
            if d is None:
                d = {(s, t): over(columns[s][at], k + t) for s in range(b) for t in range(s, b)}
            w = dict(d)
            if not last:
                then = (k + b - first) // 8
                for s in range(b):
                    for t in range(b):
                        w[s, b + t] = over(columns[s][then], k + b + t)
                    ahead = jnp.broadcast_to(
                        tiles[then][:, k + b + s : k + b + s + 1], (8, n)
                    )
                    for t in range(s, b):
                        w[b + s, b + t] = over(ahead, k + b + t)
            inside = (lane >= k) & (lane < k + b)
            rows = [
                jnp.where(lane == k + s, 1.0, jnp.where(inside, 0.0, over(tiles[at], off + s)))
                for s in range(b)
            ]
            size = b if last else 2 * b
            w1, turned, (i00, i01, i11), r1 = eliminate(w, 0, size)
            w2, _, (j00, j01, j11), _ = eliminate(w1, 2, size)
            n0 = i00 * rows[0] + i01 * rows[1]
            n1 = i01 * rows[0] + i11 * rows[1]
            m2 = rows[2] - (w[0, 2] * n0 + w[1, 2] * n1)
            m3 = rows[3] - (w[0, 3] * n0 + w[1, 3] * n1)
            n2 = j00 * m2 + j01 * m3
            n3 = j01 * m2 + j11 * m3
            n0 = n0 - (turned[2][0] * r1 * n2 + turned[3][0] * r1 * n3)
            n1 = n1 - (turned[2][1] * r1 * n2 + turned[3][1] * r1 * n3)
            new = [n0, n1, n2, n3]
            if not last:
                d = {(s, t): w2[b + s, b + t] for s in range(b) for t in range(s, b)}
            after = []
            for i, tile in enumerate(tiles):
                c = [columns[s][i] for s in range(b)]
                left = jnp.where(inside, 0.0, tile) - (
                    (c[0] * n0 + c[1] * n1) + (c[2] * n2 + c[3] * n3)
                )
                if i == at:
                    for s in range(b):
                        left = jnp.where(sub == off + s, new[s], left)
                after.append(left)
            tiles = after
        r = jnp.concatenate(tiles, 0)
        inside_n = (lane_n >= first) & (lane_n < first + h)
        rest = jnp.where(inside_n, 0.0, a) - jnp.dot(
            a[:, first : first + h], r, precision=highest, preferred_element_type=f32
        )
        pieces = ([rest[:first]] if first else []) + [r]
        a = jnp.concatenate(pieces + ([rest[first + h :]] if first + h < n else []), 0)
    return a


def block_step(k, p, a, d, left, r):
    n = 128
    row = lax.broadcasted_iota(jnp.int32, (n, n), 0)
    column = lax.broadcasted_iota(jnp.int32, (n, n), 1)
    eye = jnp.where(row == column, 1.0, 0.0)
    at = pl.ds(pl.multiple_of(k * n, n), n)
    then = pl.ds(pl.multiple_of(jnp.minimum(k + 1, kept // n - 1) * n, n), n)
    a[at, at] = -eye
    left[...] = a[:, at]
    a[:, at] = jnp.zeros((kept, n), f32)
    a[at, at] = eye
    r[...] = jnp.dot(p, a[at, :], precision=highest, preferred_element_type=f32)
    a[at, :] = jnp.zeros((n, kept), f32)
    d[...] = a[then, then] - jnp.dot(
        left[then, :], r[:, then], precision=highest, preferred_element_type=f32
    )


def update(a, left, r):
    a[...] -= jnp.dot(left[...], r[...], precision=highest, preferred_element_type=f32)


def mix(keys, q):
    s = lax.dot_general(
        keys[...], q[...], (((1,), (1,)), ((), ())), preferred_element_type=f32
    )
    e = jnp.exp((s - jnp.max(s, axis=0, keepdims=True)) * scale)
    return e / jnp.sum(e, axis=0, keepdims=True)


def gram_kernel(
    flag_ref, index_ref, packets_ref, dense_ref, slot, keys, q_ref, a, d, left, r, dense, mixing
):
    head = spread_index()[0]
    index = index_ref[pl.ds(head, 1), :]
    holder = jnp.broadcast_to(index >> 11, (width, kept))
    down = holder.T
    row = lax.broadcasted_iota(jnp.int32, (kept, width), 0)
    lane = lax.broadcasted_iota(jnp.int32, (kept, width), 1)
    same = jnp.zeros((kept, width), f32)
    for g in range(kept // width):
        across = holder[:1, g * width : (g + 1) * width]
        same += jnp.where((down == across) & (lane + g * width < row), 1.0, 0.0)
    rank = jnp.sum(same, axis=1, keepdims=True)
    own = (down & 15) * 4 + ((down >> 4) ^ head)
    slot[...] = (own * slots).astype(f32) + rank
    sent = packets_ref[:, heads_here:].astype(f32).reshape(count_rows * slots, width).astype(bf16)
    keys[...] = jnp.dot(
        one_hot((down * slots).astype(f32) + rank, count_rows * slots),
        sent,
        preferred_element_type=f32,
    ).astype(bf16)

    @pl.when(flag_ref[0] > 0)
    def _():
        pltpu.sync_copy(dense_ref, dense)
        keys[...] = dense[:, :width]
        slot[...] = dense[:, width:].astype(f32)

    q_ref[...] = packets_ref[:, head].astype(f32).reshape(kept, width).astype(bf16)
    mixing[...] = mix(keys, q_ref)
    row = lax.broadcasted_iota(jnp.int32, (kept, kept), 0)
    column = lax.broadcasted_iota(jnp.int32, (kept, kept), 1)
    a[...] = lax.dot_general(
        mixing[...],
        mixing[...],
        (((1,), (1,)), ((), ())),
        precision=highest,
        preferred_element_type=f32,
    ) + jnp.where(row == column, ridge_weight, 0.0)
    n = 128
    block_step(jnp.int32(0), invert_block(a[:n, :n], n, panel, 0, n), a, d, left, r)
    update(a, left, r)
    d[...] = invert_block(d[...], n, 32, 0, 96)


def gram(flag, kept_index, packets, dense):
    n = 128
    return call(
        gram_kernel,
        "gram",
        (
            shape((kept, width), f32),
            shape((kept, width), bf16),
            shape((count_rows * group, width), bf16),
            shape((kept, kept), f32),
            shape((n, n), f32),
        ),
        in_specs=[whole_smem] + [whole_vmem] * 2 + [whole_any],
        out_specs=[whole_vmem] * 5,
        scratch_shapes=[
            pltpu.VMEM((kept, n), f32),
            pltpu.VMEM((n, kept), f32),
            pltpu.VMEM((kept, 2 * width), bf16),
            pltpu.VMEM((kept, kept), f32),
        ],
        cost_estimate=pl.CostEstimate(
            flops=10**10, bytes_accessed=6 * 2**20, transcendentals=2**18
        ),
        compiler_params=params(24),
    )(flag, kept_index, packets, dense)


def in_pieces(x):
    high = x.astype(bf16)
    rest = x - high.astype(f32)
    middle = rest.astype(bf16)
    low = (rest - middle.astype(f32)).astype(bf16)
    return jnp.concatenate([high, middle, low], 0)


def weigh_kernel(
    flag_ref, slot, keys, q, a_ref, d_ref,
    weight_ref, share_ref, plain_ref, a, d, left, r, mixing,
):
    mixing[...] = mix(keys, q)
    n = 128
    block_step(jnp.int32(1), invert_block(d_ref[...], n, 32, 96, n), a, d, left, r)

    def step(k, _):
        update(a, left, r)
        block_step(k, invert_block(d[...], n, panel, 0, n), a, d, left, r)
        return 0

    lax.fori_loop(2, kept // n, step, 0)
    plane, own = spread_index()
    rows = [pl.ds(pl.multiple_of(128 * (plane ^ k) + 8 * own, 8), 8) for k in range(4)]
    picked = jnp.concatenate([a[at, :] for at in rows], 0)
    picked -= jnp.dot(
        jnp.concatenate([left[at, :] for at in rows], 0),
        r[...],
        precision=highest,
        preferred_element_type=f32,
    )
    weight_ref[...] = in_pieces(
        jnp.dot(picked, mixing[...], precision=highest, preferred_element_type=f32)
    )

    @pl.when(flag_ref[0] == 0)
    def _():
        hot = one_hot(slot[...], count_rows * slots)
        share_ref[...] = jnp.dot(
            in_pieces(ridge_weight * picked), hot, preferred_element_type=f32
        ).astype(bf16)
        plain_ref[...] = jnp.zeros(plain_ref.shape, f32)

    @pl.when(flag_ref[0] > 0)
    def _():
        share_ref[...] = jnp.zeros(share_ref.shape, bf16)
        plain_ref[...] = jnp.dot(
            ridge_weight * picked, slot[...], precision=highest, preferred_element_type=f32
        )


def weigh(flag, *state):
    n = 128
    return call(
        weigh_kernel,
        "weigh",
        (
            shape((96, kept), bf16),
            shape((96, count_rows * slots), bf16),
            shape((32, width), f32),
            shape((kept, kept), f32),
        ),
        in_specs=[whole_smem] + [whole_vmem] * 5,
        out_specs=[whole_vmem] * 4,
        input_output_aliases={4: 3},
        scratch_shapes=[
            pltpu.VMEM((n, n), f32),
            pltpu.VMEM((kept, n), f32),
            pltpu.VMEM((n, kept), f32),
            pltpu.VMEM((kept, kept), f32),
        ],
        cost_estimate=pl.CostEstimate(
            flops=2 * 10**10, bytes_accessed=6 * 2**20, transcendentals=0
        ),
        compiler_params=params(20),
    )(flag, *state)[:3]


def finish_kernel(weight_ref, share_ref, plain_ref, full_ref, sent_ref, *out_refs):
    sent = sent_ref[...].astype(f32)
    targets = [
        jnp.concatenate(
            [sent[:, 4 * i + x].reshape(16 * group, width) for x in range(4)], 0
        )
        for i in range(2)
    ]
    values = sent[:, 8:].reshape(count_rows * slots, width).astype(bf16)
    fitted = jnp.dot(
        weight_ref[...], jnp.concatenate(targets, 1).astype(bf16), preferred_element_type=f32
    )
    shared = jnp.dot(share_ref[...], values, preferred_element_type=f32)
    total = fitted[:, :width] + fitted[:, width:] + shared
    total = total[:32] + total[32:64] + total[64:] + plain_ref[...]
    plane = spread_index()[0]
    for k, out_ref in enumerate(out_refs):
        out_ref[:8] = total[8 * k : 8 * k + 8]
        out_ref[8:] = full_ref[plane ^ k]


def finish(weight, share, plain, full, sent):
    return call(
        finish_kernel,
        "finish",
        [shape((16, width), f32)] * 4,
        in_specs=[whole_vmem] * 5,
        out_specs=[whole_vmem] * 4,
        cost_estimate=pl.CostEstimate(
            flops=2 * 96 * 2560 * 256, bytes_accessed=2**20, transcendentals=0
        ),
        compiler_params=params(10),
    )(weight, share, plain, full, sent)


def arrange_kernel(b0_ref, b1_ref, b2_ref, b3_ref, out_ref, fitted_ref):
    plane = spread_index()[0]
    for k, ref in enumerate((b0_ref, b1_ref, b2_ref, b3_ref)):
        fitted_ref[plane ^ k] = ref[:8]
        out_ref[plane ^ k] = ref[8:].astype(bf16)


def arrange(blocks):
    return call(
        arrange_kernel,
        "arrange",
        (shape((heads_here, group, width), bf16), shape((heads_here, 8, width), f32)),
        in_specs=[whole_vmem] * 4,
        out_specs=[whole_vmem] * 2,
        cost_estimate=pl.CostEstimate(flops=2**13, bytes_accessed=2**16, transcendentals=0),
        compiler_params=params(4),
    )(*blocks)


def dense_rows(kept_index, cache_keys, cache_values):
    local_index = kept_index - own_base()
    inside = (local_index >= 0) & (local_index < local_len)
    at = jnp.clip(local_index, 0, local_len - 1)
    head = jnp.arange(heads_here, dtype=jnp.int32)[:, None]
    rows = jnp.concatenate([cache_keys[at, head], cache_values[at, head]], -1)
    rows = jnp.where(inside[..., None], rows, 0).reshape(count_rows, 32, 2 * width)
    parts = lax.all_to_all(rows, seq_axes, 0, 0)
    found = jnp.sum(parts.astype(f32), axis=0).astype(bf16)
    found = jnp.broadcast_to(found[None], (16,) + found.shape)
    return lax.all_to_all(found, ("y", "z"), 0, 0).reshape(kept, 2 * width)


def along_x(blocks):
    return [blocks[0]] + [
        lax.ppermute(blocks[k], "x", [(i, i ^ k) for i in range(4)]) for k in range(1, 4)
    ]


def on_device(ref_queries, query_pos, cache_keys, cache_values, kept_index):
    keys = cache_keys.reshape(local_len * heads_here, width)
    values = cache_values.reshape(local_len * heads_here, width)
    packets, *kept_values = pack(
        query_pos, kept_index, ref_queries.reshape(heads_here, group, width), keys, values
    )
    packets = lax.all_to_all(packets, seq_axes, 0, 0)
    kept_values = along_x(kept_values)
    parts, flag = attend(packets, keys, values)
    parts = lax.all_to_all(parts, seq_axes, 0, 0)
    dense = lax.cond(
        flag[0] > 0,
        dense_rows,
        lambda *_: jnp.zeros((kept, 2 * width), bf16),
        kept_index,
        cache_keys,
        cache_values,
    )
    state = gram(flag, kept_index, packets, dense)
    full, sent = combine(parts, kept_values)
    sent = lax.all_to_all(sent, ("y", "z"), 0, 0)
    out, fitted = arrange(along_x(finish(*weigh(flag, *state), full, sent)))
    return (out.reshape(1, heads_here * group, width), fitted)


def solution(mesh):
    split = Mesh(mesh.devices.reshape(4, 4, 4, 2), seq_axes + ("head",))
    in_specs = (
        P(seq_axes, "head", None),
        P(seq_axes),
        P(seq_axes, "head", None),
        P(seq_axes, "head", None),
        P("head", None),
    )
    out_specs = (P(seq_axes, "head", None), P("head", seq_axes, None))
    return jax.shard_map(
        on_device, mesh=split, in_specs=in_specs, out_specs=out_specs, check_vma=False
    )
```
